256 devices in a mesh: member: 16 (over y, z_lo), grid: 16 (over z_hi, x, core).
Axes of the slice: x: 4, y: 4, z: 8 (z_hi: 2, z_lo: 4; z = z_hi * 4 + z_lo), core: 2. Of those that a mesh axis runs over, the one named last changes fastest.
Arguments:
- latents: bfloat16 [16, 16384, 1024], P('member', 'grid'), may hold values from -6 to 6
- w_in: bfloat16 [1024, 1024], replicated, may hold values from -0.1875 to 0.1875
- b_in: float32 [1024], replicated, may hold values from -3 to 3
- w_out: bfloat16 [1024, 96], replicated, may hold values from -0.1875 to 0.1875
- b_out: float32 [96], replicated, may hold values from -3 to 3
- target: float32 [96, 16384], P('member', 'grid'), may hold values from -6 to 6
- area_weight: float32 [16384], P('grid'), may hold values from 0.25 to 10
- var_weight: float32 [96], P('member'), may hold values from 0.25 to 10
- smoothers: float32 [2, 128, 4, 128, 128], P(None, 'grid'), may hold values from -0.25 to 0.25
- block_index: int32 [2, 128, 4], P(None, 'grid'), may hold values from 0 to 127, as said below
- block_count: int32 [2, 128], P(None, 'grid'), may hold values from 1 to 4, as said below
Outputs:
- grad_latent: bfloat16 [16, 16384, 1024], P('member', 'grid')
- loss: float32 [], replicated
The draws below stay inside these ranges and needn't reach their ends.
Inputs may be any that keep to these rules, and one draw needn't show every extreme that they name: `block_index`: block row r lists blocks that lie at most 8 blocks from r on either side; that distance is reached on both sides in some rows; entries of a row may repeat. Only the first block_count[s, r] slots of block row r are used.
All inputs are finite; a program needn't handle non-finite values.
Results may differ from the reference program's by a relative error of at most 0.008.
Values may be sent and summed in bfloat16 or wider, within the bound.
A program may use at most 64 MiB of HBM per device.

```python
import functools
import math
import jax
import jax.numpy as jnp
from jax import lax

LATENT = 1024
FFN_WIDTH = 1024
VARS = 96
MEMBERS = 16
SCALES = 2
BLOCK = 128
KMAX = 4
PTS_DEV = 1024
NPTS = 16384
NBLK = 128


def draw_block_index(key, part):
    key = jax.random.fold_in(key, 11)
    reach = PTS_DEV // BLOCK
    rows = jnp.arange(NBLK, dtype=jnp.int32)
    lowest = jnp.maximum(rows - reach, 0)[None, :, None]
    upmost = jnp.minimum(rows + reach, NBLK - 1)[None, :, None]
    offset = jax.random.randint(key, (SCALES, NBLK, KMAX), 0, 2 * reach + 1, dtype=jnp.int32)
    picked = jnp.clip(rows[None, :, None] - reach + offset, lowest, upmost)
    slot = jnp.arange(KMAX, dtype=jnp.int32)[None, None, :]
    forced = (rows % 3 == 1)[None, :, None]
    picked = jnp.where(forced & (slot == 0), lowest, picked)
    picked = jnp.where(forced & (slot == 1), upmost, picked)
    return picked.astype(jnp.int32)


def draw_block_count(key, part):
    key = jax.random.fold_in(key, 23)
    rows = jnp.arange(NBLK, dtype=jnp.int32)
    counts = jax.random.randint(key, (SCALES, NBLK), 1, KMAX + 1, dtype=jnp.int32)
    counts = jnp.where((rows % 3 == 1)[None, :], KMAX, counts)
    return counts.astype(jnp.int32)


def draw_area_weight(key, part):
    key = jax.random.fold_in(key, 31)
    place = jnp.arange(NPTS, dtype=jnp.float32) / max(NPTS - 1, 1)
    noise = jnp.exp(jax.random.uniform(key, (NPTS,), jnp.float32, math.log(0.3), math.log(3.0)))
    ramp = 1.0 + 2.0 * place
    return (noise * ramp).astype(jnp.float32)


def draw_var_weight(key, part):
    key = jax.random.fold_in(key, 37)
    place = jnp.arange(VARS, dtype=jnp.float32) / max(VARS - 1, 1)
    noise = jnp.exp(jax.random.uniform(key, (VARS,), jnp.float32, math.log(0.3), math.log(3.0)))
    ramp = 1.0 + 2.0 * place
    return (noise * ramp).astype(jnp.float32)


def block_levels(own_key, dims, cuts, low, largest):
    level = 1.0
    for axis_at, parts in cuts:
        steps = jax.random.uniform(jax.random.fold_in(jax.random.fold_in(own_key, 6), axis_at), (parts,), jnp.float32, low / len(cuts), largest / len(cuts))
        level = level * jnp.repeat(jnp.exp(steps), dims[axis_at] // parts).reshape((-1,) + (1,) * (len(dims) - 1 - axis_at))
    return level


def bell_draw(rng, extent, scale, bound, shards=(), kind=jnp.bfloat16):
    values = jax.random.normal(rng, extent, jnp.float32) * scale
    if len(shards) > 0:
        values = block_levels(rng, extent, shards, -0.22, 0.18) * values
    return jnp.clip(values, min=-bound, max=bound).astype(kind)


def setup_inputs(seed: int = 0) -> dict:
    streams_of = jax.random.split(jax.random.key(seed), 12)
    return {
        "latents": bell_draw(streams_of[0], (MEMBERS, NPTS, LATENT), 1.0, 6.0, ((0, 16), (1, 16))),
        "w_in": bell_draw(streams_of[1], (LATENT, FFN_WIDTH), LATENT ** -0.5, 0.1875),
        "b_in": bell_draw(streams_of[2], (FFN_WIDTH,), 0.5, 3.0, (), jnp.float32),
        "w_out": bell_draw(streams_of[3], (FFN_WIDTH, VARS), FFN_WIDTH ** -0.5, 0.1875),
        "b_out": bell_draw(streams_of[4], (VARS,), 0.5, 3.0, (), jnp.float32),
        "target": bell_draw(streams_of[5], (VARS, NPTS), 1.0, 6.0, ((0, 16), (1, 16)), jnp.float32),
        "area_weight": draw_area_weight(jax.random.fold_in(streams_of[11], 71), 0),
        "var_weight": draw_var_weight(jax.random.fold_in(streams_of[11], 71), 0),
        "smoothers": bell_draw(streams_of[8], (SCALES, NBLK, KMAX, BLOCK, BLOCK), (KMAX * BLOCK) ** -0.5, 0.25, ((1, 16),), jnp.float32),
        "block_index": draw_block_index(jax.random.fold_in(streams_of[11], 71), 0),
        "block_count": draw_block_count(jax.random.fold_in(streams_of[11], 71), 0),
    }


kernel_eps = 0.01
highest = lax.Precision.HIGHEST

def wide_dot(left, right):
    return jnp.dot(left.astype(jnp.float32), right.astype(jnp.float32), precision=highest, preferred_element_type=jnp.float32)

def mask_weights(smoother, counts):
    live = (jnp.arange(KMAX, dtype=jnp.int32)[None, :] < counts[:, None]).astype(jnp.float32)
    return smoother * live[:, :, None, None]

def smooth_global(field_rows, masked, indices):
    height = field_rows.shape[0]
    blocks = field_rows.reshape(height, NBLK, BLOCK)
    picked = jnp.take(blocks, indices, axis=1)
    result = jnp.einsum('rbkp,bkpq->rbq', picked, masked, precision=highest)
    return result.reshape(height, NPTS)

def adjoint_global(grad_rows, masked, indices):
    height = grad_rows.shape[0]
    blocks = grad_rows.reshape(height, NBLK, BLOCK)
    contrib = jnp.einsum('rbq,bkpq->rbkp', blocks, masked, precision=highest)
    onehot = (indices[:, :, None] == jnp.arange(NBLK, dtype=jnp.int32)[None, None, :]).astype(jnp.float32)
    result = jnp.einsum('rbkp,bkc->rcp', contrib, onehot, precision=highest)
    return result.reshape(height, NPTS)

def ensemble_loss(fields, truth, weight_grid):
    members = fields.shape[0]
    spread = fields[:, None] - fields[None, :]
    kernel = jnp.sqrt(spread * spread + kernel_eps)
    miss = fields - truth[None]
    kernel_miss = jnp.sqrt(miss * miss + kernel_eps)
    score = lax.optimization_barrier(jnp.mean(kernel_miss, 0)) - (lax.optimization_barrier(jnp.sum(kernel, (0, 1))) - members * math.sqrt(kernel_eps)) / (2.0 * members * (members - 1))
    total = jnp.sum(weight_grid * score)
    grad = weight_grid[None] * (miss / kernel_miss - lax.optimization_barrier(jnp.sum(spread / kernel, 1)) / (members - 1))
    return (total, grad)

def score_variable(packed):
    return ensemble_loss(packed[0], packed[1], packed[2])

def reference(latents, w_in, b_in, w_out, b_out, target, area_weight, var_weight, smoothers, block_index, block_count):

    def forward(latent_rows):
        pre_act = wide_dot(latent_rows, w_in) + b_in
        hidden = jax.nn.gelu(pre_act).astype(jnp.bfloat16)
        return wide_dot(hidden, w_out).T + b_out[:, None]
    predicted = lax.map(forward, latents)
    rounded = lax.optimization_barrier(predicted.astype(jnp.bfloat16)).astype(jnp.float32)
    truth_round = lax.optimization_barrier(target.astype(jnp.bfloat16)).astype(jnp.float32)
    layers = [predicted]
    truths = [target]
    masks = []
    for scale in range(SCALES):
        masked = mask_weights(smoothers[scale], block_count[scale])
        masks.append(masked)
        smoother_fn = functools.partial(smooth_global, masked=masked, indices=block_index[scale])
        layers.append(lax.map(smoother_fn, rounded))
        truths.append(smooth_global(truth_round, masked, block_index[scale]))
    weight_grid = var_weight[:, None] * area_weight[None, :]
    total = jnp.zeros((), jnp.float32)
    layer_grads = []
    for layer_field, layer_truth in zip(layers, truths):
        totals, grads = lax.map(score_variable, (jnp.swapaxes(layer_field, 0, 1), layer_truth, weight_grid))
        total = total + jnp.sum(totals)
        layer_grads.append(jnp.swapaxes(grads, 0, 1))
    field_grad = layer_grads[0]
    for scale in range(SCALES):
        adjoint_fn = functools.partial(adjoint_global, masked=masks[scale], indices=block_index[scale])
        field_grad = field_grad + lax.map(adjoint_fn, layer_grads[scale + 1])

    def backward(packed):
        latent_rows, grad_rows = packed
        pre_act = wide_dot(latent_rows, w_in) + b_in
        _, gelu_back = jax.vjp(jax.nn.gelu, pre_act)
        grad_round = lax.optimization_barrier(grad_rows.astype(jnp.bfloat16))
        hidden_grad = wide_dot(grad_round.T, w_out.T)
        pre_grad = lax.optimization_barrier(gelu_back(hidden_grad)[0].astype(jnp.bfloat16))
        return wide_dot(pre_grad, w_in.T).astype(jnp.bfloat16)
    grad_latent = lax.map(backward, (latents, field_grad))
    loss = total / ((SCALES + 1) * VARS * NPTS)
    return (grad_latent, loss)
```

```python
import functools

import jax
import jax.numpy as jnp
from jax import lax
from jax.experimental import pallas as pl
from jax.experimental.pallas import tpu as pltpu
from jax.sharding import PartitionSpec as P

MESH = pl.DeviceIdType.MESH
F32 = jnp.float32
BF16 = jnp.bfloat16
EPS = 0.01
LANE = 128
NB = 8
SLOTS = 64
VD = 6
MEM = 16
CH = VD * NB
ROWS = MEM * CH
ALL = ROWS + CH
PAD = 112
T_ORDER, T_FLAG, T_LAST, T_VALID, T_POS, T_LIVE, T_SIZE = 0, 64, 128, 152, 192, 256, 320


def slot_table(bi, bc, tab, cnt, first):
    base = (lax.axis_index("grid") - 1) * NB

    def clear(c, _):
        cnt[c] = 0
        return 0

    lax.fori_loop(0, 3 * NB, clear, 0)

    def count(i, _):
        s, r, k = i // (NB * 4), (i // 4) % NB, i % 4
        pos = jnp.clip(bi[s, r, k] - base, 0, 3 * NB - 1)
        tab[T_POS + i] = pos
        tab[T_LIVE + i] = (k < bc[s, r]).astype(jnp.int32)
        cnt[pos] = cnt[pos] + 1
        return 0

    lax.fori_loop(0, SLOTS, count, 0)

    def starts(c, run):
        n = cnt[c]
        tab[T_VALID + c] = jnp.minimum(n, 1)
        tab[T_LAST + c] = jnp.maximum(run + n - 1, 0)
        cnt[c] = run
        first[c] = run
        return run + n

    lax.fori_loop(0, 3 * NB, starts, jnp.int32(0))

    def place(i, _):
        pos = tab[T_POS + i]
        t = cnt[pos]
        cnt[pos] = t + 1
        tab[T_ORDER + t] = i
        tab[T_FLAG + t] = (t != first[pos]).astype(jnp.int32)
        return 0

    lax.fori_loop(0, SLOTS, place, 0)


def forward_kernel(bi, bc, lat, w_in, b_in, w_out, b_out, field, slope, tab, pf, cnt, first):
    i = pl.program_id(0)
    rows = lat.shape[0]

    @pl.when(i == 0)
    def _():
        slot_table(bi, bc, tab, cnt, first)

    x = lat[...]
    pred = jnp.zeros((rows, w_out.shape[1]), F32)
    step = 256
    c = 0.7978845608028654
    a = 0.044715
    for n in range(0, w_in.shape[1], step):
        z = jnp.dot(x, w_in[:, n : n + step], preferred_element_type=F32) + b_in[:, n : n + step]
        zz = z * z
        t = jnp.tanh(z * (c + (c * a) * zz))
        half = 0.5 + 0.5 * t
        hidden = (z * half).astype(BF16)
        d = half + (0.5 * z) * (1.0 - t * t) * (c + (3.0 * c * a) * zz)
        slope[:, n : n + step] = d.astype(BF16)
        pred += jnp.dot(hidden, w_out[n : n + step, :], preferred_element_type=F32)
    flipped = (pred + b_out[...]).T
    for b in range(rows // LANE):
        pf[pl.ds(i * (rows // LANE) + b, 96, stride=NB), :] = flipped[:, b * LANE : (b + 1) * LANE]

    @pl.when(i == pl.num_programs(0) - 1)
    def _():
        field[...] = pf[...].astype(BF16).reshape(field.shape)


def backward_kernel(z, slope, w_out, w_in, out, zf):
    i = pl.program_id(0)
    rows = slope.shape[0]

    @pl.when(i == 0)
    def _():
        zf[...] = z[...].reshape(zf.shape).astype(F32)

    parts = []
    for b in range(rows // LANE):
        parts.append(zf[pl.ds(i * (rows // LANE) + b, 96, stride=NB), :].T.astype(BF16))
    g = jnp.concatenate(parts, axis=0)
    nt = (((1,), (1,)), ((), ()))
    step = 256
    pre = []
    for n in range(0, w_in.shape[1], step):
        h = lax.dot_general(g, w_out[n : n + step, :], nt, preferred_element_type=F32)
        pre.append((h * slope[:, n : n + step].astype(F32)).astype(BF16))
    pre = jnp.concatenate(pre, axis=1)
    out[...] = lax.dot_general(pre, w_in[...], nt, preferred_element_type=F32).astype(BF16)


def score_rows(layer, v, xs, area, varw, gr, total):
    w = area[...] * varw[v]
    row = layer * ALL + v * NB

    def at(m):
        return xs[pl.ds(pl.multiple_of(row + m * CH, 8), 8), :]

    y = at(MEM)
    x = [at(m) for m in range(MEM)]
    spread = [jnp.zeros((8, LANE), F32) for _ in range(MEM)]
    pairs = jnp.zeros((8, LANE), F32)
    for m in range(MEM):
        for n in range(m + 1, MEM):
            d = x[m] - x[n]
            q = d * d + EPS
            r = lax.rsqrt(q)
            u = d * r
            pairs += q * r
            spread[m] += u
            spread[n] -= u
    misses = jnp.zeros((8, LANE), F32)
    for m in range(MEM):
        d = x[m] - y
        q = d * d + EPS
        r = lax.rsqrt(q)
        misses += q * r
        g = w * (d * r - spread[m] * (1.0 / (MEM - 1)))
        gr[pl.ds(pl.multiple_of(layer * ROWS + m * CH + v * NB, 8), 8), :] = g
    return total + w * (misses * (1.0 / MEM) - pairs * (1.0 / (MEM * (MEM - 1))))


def exchange_kernel(
    tab, varw, field, target, area, smoothers, z, part,
    recv, xs, blocks, mf, mb, gr, contrib, runs, ext, rimsend, rimrecv, fsend,
    load_sem, own_sem, send_sem, recv_sem, hsend_sem, hrecv_sem,
    rsend_sem, rrecv_sem, zsend_sem, zrecv_sem,
):
    me = lax.axis_index("member")
    g = lax.axis_index("grid")
    has_low = g > 0
    has_high = g < MEM - 1
    barrier = pltpu.get_barrier_semaphore()

    def greet(i, _):
        peer = lax.rem(me + i, MEM)
        pl.semaphore_signal(barrier, inc=1, device_id=(peer, g), device_id_type=MESH)
        return 0

    lax.fori_loop(1, MEM, greet, 0)

    @pl.when(has_low)
    def _():
        pl.semaphore_signal(barrier, inc=1, device_id=(me, g - 1), device_id_type=MESH)

    @pl.when(has_high)
    def _():
        pl.semaphore_signal(barrier, inc=1, device_id=(me, g + 1), device_id_type=MESH)

    load = pltpu.make_async_copy(smoothers, mf, load_sem)
    load.start()
    own = pltpu.make_async_copy(field.at[me], recv.at[1, me], own_sem.at[0])
    own.start()

    for b in range(NB):
        xs[pl.ds(ROWS + b, VD, stride=NB), :] = target[:, b * LANE : (b + 1) * LANE]
    recv[1, MEM] = xs[ROWS:ALL, :].astype(BF16)

    @pl.when(jnp.logical_not(has_low))
    def _():
        recv[0] = jnp.zeros(recv.shape[1:], BF16)
        rimrecv[0] = jnp.zeros(rimrecv.shape[1:], BF16)

    @pl.when(jnp.logical_not(has_high))
    def _():
        recv[2] = jnp.zeros(recv.shape[1:], BF16)
        rimrecv[1] = jnp.zeros(rimrecv.shape[1:], BF16)

    pl.semaphore_wait(
        barrier, MEM - 1 + has_low.astype(jnp.int32) + has_high.astype(jnp.int32)
    )

    def to_member(i):
        peer = lax.rem(me + i, MEM)
        return pltpu.make_async_remote_copy(
            src_ref=field.at[peer], dst_ref=recv.at[1, me],
            send_sem=send_sem.at[i], recv_sem=recv_sem.at[i],
            device_id=(peer, g), device_id_type=MESH,
        )

    def from_member(i):
        src = lax.rem(me + MEM - i, MEM)
        return pltpu.make_async_remote_copy(
            src_ref=field.at[src], dst_ref=recv.at[1, src],
            send_sem=send_sem.at[i], recv_sem=recv_sem.at[i],
            device_id=(src, g), device_id_type=MESH,
        )

    def halo(i, chunk, up):
        side, there = (0, g + 1) if up else (1, g - 1)
        return pltpu.make_async_remote_copy(
            src_ref=recv.at[1, chunk], dst_ref=recv.at[0 if up else 2, chunk],
            send_sem=hsend_sem.at[side, i], recv_sem=hrecv_sem.at[side, i],
            device_id=(me, there), device_id_type=MESH,
        )

    def pass_on(i, chunk):
        @pl.when(has_high)
        def _():
            halo(i, chunk, True).start()

        @pl.when(has_low)
        def _():
            halo(i, chunk, False).start()

    def send(i, _):
        to_member(i).start()
        return 0

    lax.fori_loop(1, MEM, send, 0)
    pass_on(MEM, MEM)
    own.wait()
    pass_on(0, me)

    load.wait()

    def weights(i, _):
        live = tab[T_LIVE + i].astype(F32)
        mb[i] = (mf[i // 32, (i // 4) % NB, i % 4] * live).astype(BF16)
        return 0

    lax.fori_loop(0, SLOTS, weights, 0)

    def arrive(i, _):
        from_member(i).wait_recv()
        pass_on(i, lax.rem(me + MEM - i, MEM))
        return 0

    lax.fori_loop(1, MEM, arrive, 0)

    xs[0:ROWS, :] = recv[1, 0:MEM].reshape(ROWS, LANE).astype(F32)
    fill = jnp.zeros((PAD - 102, LANE), BF16)
    for b in range(NB):
        blocks[NB + b] = jnp.concatenate(
            [xs[pl.ds(b, 102, stride=NB), :].astype(BF16), fill], axis=0
        )
    total = lax.fori_loop(
        0, VD, lambda v, t: score_rows(0, v, xs, area, varw, gr, t), jnp.zeros((8, LANE), F32)
    )

    def landed(i, _):
        chunk = jnp.where(i == MEM, MEM, lax.rem(me + MEM - i + MEM, MEM))

        @pl.when(has_low)
        def _():
            halo(i, chunk, True).wait_recv()

        @pl.when(has_high)
        def _():
            halo(i, chunk, False).wait_recv()

        return 0

    lax.fori_loop(0, MEM + 1, landed, 0)
    for side, first in ((0, 0), (2, 2 * NB)):
        ext[0:ALL, :] = recv[side].reshape(ALL, LANE).astype(F32)
        for b in range(NB):
            blocks[first + b] = jnp.concatenate(
                [ext[pl.ds(b, 102, stride=NB), :].astype(BF16), fill], axis=0
            )

    for s in range(2):
        for r in range(NB):
            i = (s * NB + r) * 4
            picked = jnp.concatenate([blocks[tab[T_POS + i + k]] for k in range(4)], axis=1)
            res = jnp.dot(
                picked, mb[i : i + 4].reshape(4 * LANE, LANE), preferred_element_type=F32
            )
            xs[pl.ds((s + 1) * ALL + r, 102, stride=NB), :] = res[:102]

    def later(i, t):
        return score_rows(1 + i // VD, i % VD, xs, area, varw, gr, t)

    part[...] = lax.fori_loop(0, 2 * VD, later, total)

    nt = (((1,), (1,)), ((), ()))
    for s in range(2):
        for r in range(NB):
            i = (s * NB + r) * 4
            rows = gr[pl.ds((s + 1) * ROWS + r, 96, stride=NB), :].astype(BF16)
            res = lax.dot_general(
                rows, mb[i : i + 4].reshape(4 * LANE, LANE), nt, preferred_element_type=F32
            )
            for k in range(4):
                contrib[i + k] = res[:, k * LANE : (k + 1) * LANE]

    def run(t, acc):
        acc = acc * tab[T_FLAG + t].astype(F32) + contrib[tab[T_ORDER + t]]
        runs[t] = acc
        return acc

    lax.fori_loop(0, SLOTS, run, jnp.zeros((96, LANE), F32), unroll=4)
    for c in list(range(NB)) + list(range(2 * NB, 3 * NB)) + list(range(NB, 2 * NB)):
        e = runs[tab[T_LAST + c]] * tab[T_VALID + c].astype(F32)
        ext[pl.ds((c // NB) * ROWS + c % NB, 96, stride=NB), :] = e

    def rim(q, up):
        side, there = (0, g + 1) if up else (1, g - 1)
        part4 = pl.ds(q * 4, 4)
        return pltpu.make_async_remote_copy(
            src_ref=rimsend.at[side, part4], dst_ref=rimrecv.at[side, part4],
            send_sem=rsend_sem.at[side, q], recv_sem=rrecv_sem.at[side, q],
            device_id=(me, there), device_id_type=MESH,
        )

    rimsend[1] = ext[0:ROWS, :].reshape(MEM, CH, LANE).astype(BF16)

    @pl.when(has_low)
    def _():
        for q in range(4):
            rim(q, False).start()

    rimsend[0] = ext[2 * ROWS : 3 * ROWS, :].reshape(MEM, CH, LANE).astype(BF16)

    @pl.when(has_high)
    def _():
        for q in range(4):
            rim(q, True).start()

    def to_owner(i):
        peer = lax.rem(me + i, MEM)
        return pltpu.make_async_remote_copy(
            src_ref=fsend.at[peer], dst_ref=z.at[me],
            send_sem=zsend_sem.at[i], recv_sem=zrecv_sem.at[i],
            device_id=(peer, g), device_id_type=MESH,
        )

    own_z = pltpu.make_async_copy(fsend.at[me], z.at[me], own_sem.at[1])
    for q in range(4):

        @pl.when(has_low)
        def _():
            rim(q, True).wait_recv()

        @pl.when(has_high)
        def _():
            rim(q, False).wait_recv()

        for m in range(4 * q, 4 * q + 4):
            at = m * CH
            value = gr[at : at + CH, :] + ext[ROWS + at : ROWS + at + CH, :]
            value = value + (rimrecv[0, m].astype(F32) + rimrecv[1, m].astype(F32))
            fsend[m] = value.astype(BF16)
            i = lax.rem(m - me + MEM, MEM)

            @pl.when(i > 0)
            def _():
                to_owner(i).start()

            @pl.when(i == 0)
            def _():
                own_z.start()

    own_z.wait()

    def finish(i, _):
        src = lax.rem(me + MEM - i, MEM)
        pltpu.make_async_remote_copy(
            src_ref=fsend.at[src], dst_ref=z.at[src],
            send_sem=zsend_sem.at[i], recv_sem=zrecv_sem.at[i],
            device_id=(src, g), device_id_type=MESH,
        ).wait_recv()
        to_owner(i).wait_send()
        to_member(i).wait_send()
        return 0

    lax.fori_loop(1, MEM, finish, 0)

    def sent(i, _):
        @pl.when(has_high)
        def _():
            halo(i, 0, True).wait_send()

        @pl.when(has_low)
        def _():
            halo(i, 0, False).wait_send()

        return 0

    lax.fori_loop(0, MEM + 1, sent, 0)
    for q in range(4):

        @pl.when(has_high)
        def _():
            rim(q, True).wait_send()

        @pl.when(has_low)
        def _():
            rim(q, False).wait_send()


def on_device(latents, w_in, b_in, w_out, b_out, target, area_weight, var_weight,
              smoothers, block_index, block_count):
    points = latents.shape[1]
    lat = latents.reshape(points, -1)
    width = w_in.shape[1]
    tile = 256
    whole = lambda shape: pl.BlockSpec(shape, lambda i: (0,) * len(shape))
    smem = pl.BlockSpec(memory_space=pltpu.SMEM)
    vmem = pl.BlockSpec(memory_space=pltpu.VMEM)
    anywhere = pl.BlockSpec(memory_space=pl.ANY)
    field, slope, tab = pl.pallas_call(
        forward_kernel,
        grid=(points // tile,),
        out_shape=(
            jax.ShapeDtypeStruct((MEM, CH, LANE), BF16),
            jax.ShapeDtypeStruct((points, width), BF16),
            jax.ShapeDtypeStruct((T_SIZE,), jnp.int32),
        ),
        in_specs=[
            smem, smem,
            pl.BlockSpec((tile, lat.shape[1]), lambda i: (i, 0)),
            whole(w_in.shape), whole((1, width)), whole(w_out.shape), whole((1, w_out.shape[1])),
        ],
        out_specs=(
            whole((MEM, CH, LANE)),
            pl.BlockSpec((tile, width), lambda i: (i, 0)),
            smem,
        ),
        scratch_shapes=[
            pltpu.VMEM((ROWS, LANE), F32),
            pltpu.SMEM((32,), jnp.int32),
            pltpu.SMEM((32,), jnp.int32),
        ],
        compiler_params=pltpu.CompilerParams(vmem_limit_bytes=40 * 1024 * 1024),
    )(block_index, block_count, lat, w_in, b_in.reshape(1, -1), w_out, b_out.reshape(1, -1))

    dma = pltpu.SemaphoreType.DMA
    z, part = pl.pallas_call(
        exchange_kernel,
        out_shape=(
            jax.ShapeDtypeStruct((MEM, CH, LANE), BF16),
            jax.ShapeDtypeStruct((8, LANE), F32),
        ),
        in_specs=[smem, smem, anywhere, vmem, vmem, anywhere],
        out_specs=(anywhere, vmem),
        scratch_shapes=[
            pltpu.VMEM((3, MEM + 1, CH, LANE), BF16),
            pltpu.VMEM((3 * ALL, LANE), F32),
            pltpu.VMEM((3 * NB, PAD, LANE), BF16),
            pltpu.VMEM((2, NB, 4, LANE, LANE), F32),
            pltpu.VMEM((SLOTS, LANE, LANE), BF16),
            pltpu.VMEM((3 * ROWS, LANE), F32),
            pltpu.VMEM((SLOTS, 96, LANE), F32),
            pltpu.VMEM((SLOTS, 96, LANE), F32),
            pltpu.VMEM((3 * ROWS, LANE), F32),
            pltpu.VMEM((2, MEM, CH, LANE), BF16),
            pltpu.VMEM((2, MEM, CH, LANE), BF16),
            pltpu.VMEM((MEM, CH, LANE), BF16),
            dma, dma((2,)), dma((MEM,)), dma((MEM,)), dma((2, MEM + 1)), dma((2, MEM + 1)),
            dma((2, 4)), dma((2, 4)), dma((MEM,)), dma((MEM,)),
        ],
        compiler_params=pltpu.CompilerParams(
            collective_id=0, has_side_effects=True, vmem_limit_bytes=40 * 1024 * 1024
        ),
    )(tab, var_weight, field, target, area_weight.reshape(NB, LANE), smoothers)

    grad = pl.pallas_call(
        backward_kernel,
        grid=(points // tile,),
        out_shape=jax.ShapeDtypeStruct((points, lat.shape[1]), BF16),
        in_specs=[
            whole((MEM, CH, LANE)),
            pl.BlockSpec((tile, width), lambda i: (i, 0)),
            whole(w_out.shape), whole(w_in.shape),
        ],
        out_specs=pl.BlockSpec((tile, lat.shape[1]), lambda i: (i, 0)),
        scratch_shapes=[pltpu.VMEM((ROWS, LANE), F32)],
        compiler_params=pltpu.CompilerParams(vmem_limit_bytes=40 * 1024 * 1024),
    )(z, slope, w_out, w_in)
    loss = lax.psum(jnp.sum(part), ("member", "grid")) / (3 * 96 * points * MEM)
    return grad.reshape(latents.shape), loss


def solution(mesh):
    in_specs = (
        P("member", "grid", None), P(), P(), P(), P(),
        P("member", "grid"), P("grid"), P("member"),
        P(None, "grid", None, None, None), P(None, "grid", None), P(None, "grid"),
    )
    return jax.shard_map(
        on_device, mesh=mesh, in_specs=in_specs,
        out_specs=(P("member", "grid", None), P()), check_vma=False,
    )
```

```python
import functools

import jax
import jax.numpy as jnp
from jax import lax
from jax.experimental import pallas as pl
from jax.experimental.pallas import tpu as pltpu
from jax.sharding import PartitionSpec as P

MESH = pl.DeviceIdType.MESH
F32 = jnp.float32
BF16 = jnp.bfloat16
EPS = 0.01
LANE = 128
NB = 8
SLOTS = 64
VD = 6
MEM = 16
CH = VD * NB
ROWS = MEM * CH
ALL = ROWS + CH
PAD = 112
EDGE = 7
TILE = 512
NT = (((1,), (1,)), ((), ()))
ORDER, FLAG, LAST, VALID = 0, 1, 2, 3


def slot_place(bi, i):
    base = (lax.axis_index("grid") - 1) * NB
    return jnp.clip(bi[i // 32, i % 4, (i // 4) % NB] - base, 0, 3 * NB - 1)


def slot_table(bi, posv, tabv):
    def fill(i, _):
        posv[pl.ds(i, 1), :] = jnp.full((1, LANE), slot_place(bi, i), jnp.int32)
        return 0

    lax.fori_loop(0, SLOTS, fill, 0)
    pos = posv[...]
    sub = lax.broadcasted_iota(jnp.int32, (SLOTS, LANE), 0)
    lane = lax.broadcasted_iota(jnp.int32, (SLOTS, LANE), 1)
    total = lambda x: jnp.sum(x, axis=0, keepdims=True)
    across = total(jnp.where(sub == lane, pos, 0))
    key = pos * SLOTS + sub
    before = jnp.where(lane < SLOTS, (across * SLOTS + lane < key).astype(jnp.int32), 0)
    rank = jnp.sum(before, axis=1, keepdims=True)
    here = total(jnp.where(rank == lane, pos, 0))
    previous = total(jnp.where(rank + 1 == lane, pos, 0))
    tabv[ORDER : ORDER + 1, :] = total(jnp.where(rank == lane, sub, 0))
    tabv[FLAG : FLAG + 1, :] = jnp.where(lane[:1] > 0, (here == previous).astype(jnp.int32), 0)
    tabv[LAST : LAST + 1, :] = jnp.maximum(total((pos <= lane).astype(jnp.int32)) - 1, 0)
    tabv[VALID : VALID + 1, :] = jnp.minimum(total((pos == lane).astype(jnp.int32)), 1)


def score_rows(layer, v, xs, area, varw, gr, total):
    w = area[...] * varw[v]
    row = layer * ALL + v * NB

    def at(m):
        return xs[pl.ds(pl.multiple_of(row + m * CH, 8), 8), :]

    y = at(MEM)
    x = [at(m) for m in range(MEM)]
    spread = [jnp.zeros((8, LANE), F32) for _ in range(MEM)]
    pairs = jnp.zeros((8, LANE), F32)
    for m in range(MEM):
        for n in range(m + 1, MEM):
            d = x[m] - x[n]
            q = d * d + EPS
            r = lax.rsqrt(q)
            u = d * r
            pairs += q * r
            spread[m] += u
            spread[n] -= u
    misses = jnp.zeros((8, LANE), F32)
    for m in range(MEM):
        d = x[m] - y
        q = d * d + EPS
        r = lax.rsqrt(q)
        misses += q * r
        g = w * (d * r - spread[m] * (1.0 / (MEM - 1)))
        gr[pl.ds(pl.multiple_of(layer * ROWS + m * CH + v * NB, 8), 8), :] = g
    return total + w * (misses * (1.0 / MEM) - pairs * (1.0 / (MEM * (MEM - 1))))


def decoder_kernel(
    bi, bc, varw, lat, w_in, b_in, w_out, b_out, target, area, smoothers, out, loss,
    lat_v, w_v, slope, field, recv, xs, blocks, mf, mb, gr, contrib, runs, ext,
    rimsend, rimrecv, fsend, zrecv, zrim, lmem, lgrid, posv, tabv, tab,
    in_sem, out_sem, load_sem, tab_sem, send_sem, recv_sem, hsend_sem, hrecv_sem,
    rsend_sem, rrecv_sem, zsend_sem, zrecv_sem, esend_sem, erecv_sem,
    l1send_sem, l1recv_sem, l2send_sem, l2recv_sem,
):
    me = lax.axis_index("member")
    g = lax.axis_index("grid")
    has_low = g > 0
    has_high = g < MEM - 1
    at_edge = jnp.logical_or(g == EDGE, g == EDGE + 1)
    low_near = jnp.logical_and(has_low, g != EDGE + 1)
    high_near = jnp.logical_and(has_high, g != EDGE)
    across = jnp.where(g == EDGE, EDGE + 1, EDGE)
    barrier = pltpu.get_barrier_semaphore()
    width = w_v.shape[0]
    cut = width // 2

    def remote(src, dst, send, recv_, member, grid):
        return pltpu.make_async_remote_copy(
            src_ref=src, dst_ref=dst, send_sem=send, recv_sem=recv_,
            device_id=(member, grid), device_id_type=MESH,
        )

    def greet(i, _):
        peer = lax.rem(me + i, MEM)
        pl.semaphore_signal(barrier, inc=1, device_id=(peer, g), device_id_type=MESH)
        there = lax.rem(g + i, MEM)
        pl.semaphore_signal(barrier, inc=1, device_id=(me, there), device_id_type=MESH)

        @pl.when(at_edge)
        def _():
            pl.semaphore_signal(barrier, inc=1, device_id=(peer, across), device_id_type=MESH)

        return 0

    loads = []
    for n in range(2):
        loads.append((
            pltpu.make_async_copy(
                lat.at[pl.ds(n * TILE, TILE), :], lat_v.at[pl.ds(n * TILE, TILE), :], in_sem.at[2 * n]
            ),
            pltpu.make_async_copy(
                w_in.at[:, pl.ds(n * cut, cut)], w_v.at[:, pl.ds(n * cut, cut)], in_sem.at[2 * n + 1]
            ),
        ))
    for pair in loads:
        for copy in pair:
            copy.start()
    load = pltpu.make_async_copy(smoothers, mf, load_sem)
    load.start()
    lax.fori_loop(1, MEM, greet, 0)

    for b in range(NB):
        xs[pl.ds(ROWS + b, VD, stride=NB), :] = target[:, b * LANE : (b + 1) * LANE]
    recv[1, MEM] = xs[ROWS:ALL, :].astype(BF16)

    @pl.when(jnp.logical_not(has_low))
    def _():
        recv[0] = jnp.zeros(recv.shape[1:], BF16)

    @pl.when(jnp.logical_not(has_high))
    def _():
        recv[2] = jnp.zeros(recv.shape[1:], BF16)

    @pl.when(jnp.logical_not(low_near))
    def _():
        rimrecv[0] = jnp.zeros(rimrecv.shape[1:], BF16)

    @pl.when(jnp.logical_not(high_near))
    def _():
        rimrecv[1] = jnp.zeros(rimrecv.shape[1:], BF16)

    c = 0.7978845608028654
    a = 0.044715
    for copy in loads[0] + (loads[1][1],):
        copy.wait()

    def forward(i, _):
        @pl.when(i == 1)
        def _():
            loads[1][0].wait()

        rows = pl.ds(pl.multiple_of(i * TILE, TILE), TILE)
        pred = jnp.zeros((TILE, w_out.shape[0]), F32)
        for n in range(0, width, cut):
            z = jnp.dot(lat_v[rows, :], w_v[:, n : n + cut], preferred_element_type=F32)
            z = z + b_in[:, n : n + cut]
            zz = z * z
            t = jnp.tanh(z * (c + (c * a) * zz))
            half = 0.5 + 0.5 * t
            hidden = (z * half).astype(BF16)
            d = half + (0.5 * z) * (1.0 - t * t) * (c + (3.0 * c * a) * zz)
            slope[rows, n : n + cut] = d.astype(BF16)
            pred += lax.dot_general(hidden, w_out[:, n : n + cut], NT, preferred_element_type=F32)
        flipped = (pred + b_out[...]).T
        for b in range(TILE // LANE):
            ext[pl.ds(i * (TILE // LANE) + b, 96, stride=NB), :] = (
                flipped[:, b * LANE : (b + 1) * LANE]
            )
        return 0

    lax.fori_loop(0, width // TILE, forward, 0)
    field[...] = ext[0:ROWS, :].reshape(MEM, CH, LANE).astype(BF16)

    pl.semaphore_wait(barrier, 2 * (MEM - 1) + jnp.where(at_edge, MEM - 1, 0))

    def to_member(i):
        peer = lax.rem(me + i, MEM)
        return remote(field.at[peer], recv.at[1, me], send_sem.at[i], recv_sem.at[i], peer, g)

    def from_member(i):
        src = lax.rem(me + MEM - i, MEM)
        return remote(field.at[src], recv.at[1, src], send_sem.at[i], recv_sem.at[i], src, g)

    def halo(i, chunk, up):
        side, there = (0, g + 1) if up else (1, g - 1)
        return remote(
            recv.at[1, chunk], recv.at[0 if up else 2, chunk],
            hsend_sem.at[side, i], hrecv_sem.at[side, i], me, there,
        )

    def far(i, up):
        side = 0 if up else 1
        peer = lax.rem(me + i, MEM)
        return remote(
            field.at[peer], recv.at[0 if up else 2, me],
            hsend_sem.at[side, i], hrecv_sem.at[side, i], peer, across,
        )

    def far_send(i):
        @pl.when(g == EDGE)
        def _():
            far(i, True).start()

        @pl.when(g == EDGE + 1)
        def _():
            far(i, False).start()

    def pass_on(i, chunk, up_ok, down_ok):
        @pl.when(up_ok)
        def _():
            halo(i, chunk, True).start()

        @pl.when(down_ok)
        def _():
            halo(i, chunk, False).start()

    def send(i, _):
        to_member(i).start()
        far_send(i)
        return 0

    lax.fori_loop(1, MEM, send, 0)
    far_send(0)
    recv[1, me] = field[me]
    pass_on(MEM, MEM, has_high, has_low)
    pass_on(0, me, high_near, low_near)

    slot_table(bi, posv, tabv)
    tab_copy = pltpu.make_async_copy(tabv, tab, tab_sem)
    tab_copy.start()
    load.wait()

    def weights(i, _):
        live = (i % 4 < bc[i // 32, (i // 4) % NB]).astype(jnp.int32).astype(F32)
        mb[i] = (mf[i // 32, (i // 4) % NB, i % 4] * live).astype(BF16)
        return 0

    lax.fori_loop(0, SLOTS, weights, 0, unroll=4)

    def arrive(i, _):
        from_member(i).wait_recv()
        pass_on(i, lax.rem(me + MEM - i, MEM), high_near, low_near)
        return 0

    lax.fori_loop(1, MEM, arrive, 0)

    xs[0:ROWS, :] = recv[1, 0:MEM].reshape(ROWS, LANE).astype(F32)
    pad = jnp.zeros((PAD - 102, LANE), BF16)
    for b in range(NB):
        blocks[NB + b] = jnp.concatenate(
            [xs[pl.ds(b, 102, stride=NB), :].astype(BF16), pad], axis=0
        )
    partial = lax.fori_loop(
        0, VD, lambda v, t: score_rows(0, v, xs, area, varw, gr, t), jnp.zeros((8, LANE), F32)
    )
    tab_copy.wait()

    def landed(i, _):
        @pl.when(has_low)
        def _():
            halo(i, 0, True).wait_recv()

        @pl.when(has_high)
        def _():
            halo(i, 0, False).wait_recv()

        return 0

    lax.fori_loop(0, MEM + 1, landed, 0)
    for side, first in ((0, 0), (2, 2 * NB)):
        ext[0:ALL, :] = recv[side].reshape(ALL, LANE).astype(F32)
        for b in range(NB):
            blocks[first + b] = jnp.concatenate(
                [ext[pl.ds(b, 102, stride=NB), :].astype(BF16), pad], axis=0
            )

    for s in range(2):
        for r in range(NB):
            i = (s * NB + r) * 4
            picked = jnp.concatenate([blocks[slot_place(bi, i + k)] for k in range(4)], axis=1)
            res = jnp.dot(
                picked, mb[i : i + 4].reshape(4 * LANE, LANE), preferred_element_type=F32
            )
            xs[pl.ds((s + 1) * ALL + r, 102, stride=NB), :] = res[:102]

    def later(i, t):
        return score_rows(1 + i // VD, i % VD, xs, area, varw, gr, t)

    lmem[me] = lax.fori_loop(0, 2 * VD, later, partial)

    def loss_member(i):
        peer = lax.rem(me + i, MEM)
        return remote(lmem.at[me], lmem.at[me], l1send_sem.at[i], l1recv_sem.at[i], peer, g)

    def loss_grid(i):
        there = lax.rem(g + i, MEM)
        return remote(lgrid.at[g], lgrid.at[g], l2send_sem.at[i], l2recv_sem.at[i], me, there)

    def send_loss(i, _):
        loss_member(i).start()
        return 0

    lax.fori_loop(1, MEM, send_loss, 0)

    for s in range(2):
        for r in range(NB):
            i = (s * NB + r) * 4
            rows = gr[pl.ds((s + 1) * ROWS + r, 96, stride=NB), :].astype(BF16)
            res = lax.dot_general(
                rows, mb[i : i + 4].reshape(4 * LANE, LANE), NT, preferred_element_type=F32
            )
            for k in range(4):
                contrib[i + k] = res[:, k * LANE : (k + 1) * LANE]

    def run(t, acc):
        acc = acc * tab[FLAG, t].astype(F32) + contrib[tab[ORDER, t]]
        runs[t] = acc
        return acc

    lax.fori_loop(0, SLOTS, run, jnp.zeros((96, LANE), F32), unroll=4)

    def spread(first):
        for q in range(first, first + NB):
            e = runs[tab[LAST, q]] * tab[VALID, q].astype(F32)
            ext[pl.ds((q // NB) * ROWS + q % NB, 96, stride=NB), :] = e

    def rim(q, up):
        side, there = (0, g + 1) if up else (1, g - 1)
        some = pl.ds(q * 4, 4)
        return remote(
            rimsend.at[side, some], rimrecv.at[side, some],
            rsend_sem.at[side, q], rrecv_sem.at[side, q], me, there,
        )

    def far_rim(i, side):
        peer = lax.rem(me + i, MEM)
        return remote(
            rimsend.at[side, peer], zrim.at[me], esend_sem.at[i], erecv_sem.at[i], peer, across
        )

    def far_rims(side):
        def one(i, _):
            far_rim(i, side).start()
            return 0

        lax.fori_loop(0, MEM, one, 0)

    spread(0)
    rimsend[1] = ext[0:ROWS, :].reshape(MEM, CH, LANE).astype(BF16)

    @pl.when(low_near)
    def _():
        for q in range(4):
            rim(q, False).start()

    @pl.when(g == EDGE + 1)
    def _():
        far_rims(1)

    spread(2 * NB)
    rimsend[0] = ext[2 * ROWS : 3 * ROWS, :].reshape(MEM, CH, LANE).astype(BF16)

    @pl.when(high_near)
    def _():
        for q in range(4):
            rim(q, True).start()

    @pl.when(g == EDGE)
    def _():
        far_rims(0)

    spread(NB)

    def loss_arrived(i, _):
        src = lax.rem(me + MEM - i, MEM)
        remote(
            lmem.at[src], lmem.at[src], l1send_sem.at[i], l1recv_sem.at[i], src, g
        ).wait_recv()
        return 0

    lax.fori_loop(1, MEM, loss_arrived, 0)
    lgrid[g] = jnp.sum(lmem[...], axis=0)

    def send_sum(i, _):
        loss_grid(i).start()
        return 0

    lax.fori_loop(1, MEM, send_sum, 0)

    def to_owner(i):
        peer = lax.rem(me + i, MEM)
        return remote(fsend.at[peer], zrecv.at[me], zsend_sem.at[i], zrecv_sem.at[i], peer, g)

    for q in range(4):

        @pl.when(low_near)
        def _():
            rim(q, True).wait_recv()

        @pl.when(high_near)
        def _():
            rim(q, False).wait_recv()

        for m in range(4 * q, 4 * q + 4):
            at = m * CH
            value = gr[at : at + CH, :] + ext[ROWS + at : ROWS + at + CH, :]
            value = value + (rimrecv[0, m].astype(F32) + rimrecv[1, m].astype(F32))
            fsend[m] = value.astype(BF16)
            i = lax.rem(m - me + MEM, MEM)

            @pl.when(i > 0)
            def _():
                to_owner(i).start()

    zrecv[me] = fsend[me]

    def owned(i, _):
        src = lax.rem(me + MEM - i, MEM)
        remote(
            fsend.at[src], zrecv.at[src], zsend_sem.at[i], zrecv_sem.at[i], src, g
        ).wait_recv()
        return 0

    lax.fori_loop(1, MEM, owned, 0)
    ext[0:ROWS, :] = zrecv[...].reshape(ROWS, LANE).astype(F32)

    @pl.when(at_edge)
    def _():
        def one(i, _):
            src = lax.rem(me + MEM - i, MEM)
            remote(
                rimsend.at[0, src], zrim.at[src], esend_sem.at[i], erecv_sem.at[i], src, across
            ).wait_recv()
            return 0

        lax.fori_loop(0, MEM, one, 0)
        ext[0:ROWS, :] += zrim[...].reshape(ROWS, LANE).astype(F32)

    stores = [
        pltpu.make_async_copy(
            lat_v.at[pl.ds(n * TILE, TILE), :], out.at[pl.ds(n * TILE, TILE), :], out_sem.at[n]
        )
        for n in range(2)
    ]

    def backward(i, _):
        rows = pl.ds(pl.multiple_of(i * TILE, TILE), TILE)
        parts = []
        for b in range(TILE // LANE):
            parts.append(ext[pl.ds(i * (TILE // LANE) + b, 96, stride=NB), :].T.astype(BF16))
        grad = jnp.concatenate(parts, axis=0)
        pre = []
        for n in range(0, width, cut):
            h = jnp.dot(grad, w_out[:, n : n + cut], preferred_element_type=F32)
            pre.append((h * slope[rows, n : n + cut].astype(F32)).astype(BF16))
        pre = jnp.concatenate(pre, axis=1)
        lat_v[rows, :] = lax.dot_general(pre, w_v[...], NT, preferred_element_type=F32).astype(BF16)
        for n in range(2):

            @pl.when(i == n)
            def _():
                stores[n].start()

        return 0

    lax.fori_loop(0, 2, backward, 0)

    def rest(i, _):
        src = lax.rem(g + MEM - i, MEM)
        remote(
            lgrid.at[src], lgrid.at[src], l2send_sem.at[i], l2recv_sem.at[i], me, src
        ).wait_recv()
        loss_member(i).wait_send()
        loss_grid(i).wait_send()
        to_member(i).wait_send()
        to_owner(i).wait_send()
        return 0

    lax.fori_loop(1, MEM, rest, 0)
    points = lat_v.shape[0]
    loss[0, 0] = jnp.sum(jnp.sum(lgrid[...], axis=0)) * (1.0 / (3 * 96 * points * MEM))

    def sent(i, _):
        @pl.when(has_high)
        def _():
            halo(i, 0, True).wait_send()

        @pl.when(has_low)
        def _():
            halo(i, 0, False).wait_send()

        return 0

    lax.fori_loop(0, MEM + 1, sent, 0)

    @pl.when(at_edge)
    def _():
        def one(i, _):
            far_rim(i, 0).wait_send()
            return 0

        lax.fori_loop(0, MEM, one, 0)

    for q in range(4):

        @pl.when(high_near)
        def _():
            rim(q, True).wait_send()

        @pl.when(low_near)
        def _():
            rim(q, False).wait_send()

    for copy in stores:
        copy.wait()


def on_device(latents, w_in, b_in, w_out, b_out, target, area_weight, var_weight,
              smoothers, block_index, block_count):
    points = latents.shape[1]
    lat = latents.reshape(points, -1)
    width = w_in.shape[1]
    smem = pl.BlockSpec(memory_space=pltpu.SMEM)
    vmem = pl.BlockSpec(memory_space=pltpu.VMEM)
    anywhere = pl.BlockSpec(memory_space=pl.ANY)
    dma = pltpu.SemaphoreType.DMA
    some = dma((MEM,))
    chunks = (MEM, CH, LANE)
    grad, loss = pl.pallas_call(
        decoder_kernel,
        out_shape=(
            jax.ShapeDtypeStruct(lat.shape, BF16),
            jax.ShapeDtypeStruct((1, 1), F32),
        ),
        in_specs=[smem, smem, smem, anywhere, anywhere, vmem, vmem, vmem, vmem, vmem, anywhere],
        out_specs=(anywhere, smem),
        scratch_shapes=[
            pltpu.VMEM(lat.shape, BF16),
            pltpu.VMEM(w_in.shape, BF16),
            pltpu.VMEM((points, width), BF16),
            pltpu.VMEM(chunks, BF16),
            pltpu.VMEM((3, MEM + 1, CH, LANE), BF16),
            pltpu.VMEM((3 * ALL, LANE), F32),
            pltpu.VMEM((3 * NB, PAD, LANE), BF16),
            pltpu.VMEM(smoothers.shape, F32),
            pltpu.VMEM((SLOTS, LANE, LANE), BF16),
            pltpu.VMEM((3 * ROWS, LANE), F32),
            pltpu.VMEM((SLOTS, 96, LANE), F32),
            pltpu.VMEM((SLOTS, 96, LANE), F32),
            pltpu.VMEM((3 * ROWS, LANE), F32),
            pltpu.VMEM((2,) + chunks, BF16),
            pltpu.VMEM((2,) + chunks, BF16),
            pltpu.VMEM(chunks, BF16),
            pltpu.VMEM(chunks, BF16),
            pltpu.VMEM(chunks, BF16),
            pltpu.VMEM((MEM, 8, LANE), F32),
            pltpu.VMEM((MEM, 8, LANE), F32),
            pltpu.VMEM((SLOTS, LANE), jnp.int32),
            pltpu.VMEM((8, LANE), jnp.int32),
            pltpu.SMEM((8, LANE), jnp.int32),
            dma((4,)), dma((2,)), dma, dma, some, some,
            dma((2, MEM + 1)), dma((2, MEM + 1)), dma((2, 4)), dma((2, 4)),
            some, some, some, some, some, some, some, some,
        ],
        compiler_params=pltpu.CompilerParams(
            collective_id=0, has_side_effects=True, vmem_limit_bytes=60 * 1024 * 1024
        ),
    )(
        jnp.transpose(block_index, (0, 2, 1)), block_count, var_weight, lat, w_in,
        b_in.reshape(1, -1), w_out.T, b_out.reshape(1, -1), target,
        area_weight.reshape(NB, LANE), smoothers,
    )
    return grad.reshape(latents.shape), loss.reshape(())


def solution(mesh):
    in_specs = (
        P("member", "grid", None), P(), P(), P(), P(),
        P("member", "grid"), P("grid"), P("member"),
        P(None, "grid", None, None, None), P(None, "grid", None), P(None, "grid"),
    )
    return jax.shard_map(
        on_device, mesh=mesh, in_specs=in_specs,
        out_specs=(P("member", "grid", None), P()), check_vma=False,
    )
```

```python
import functools

import jax
import jax.numpy as jnp
from jax import lax
from jax.experimental import pallas as pl
from jax.experimental.pallas import tpu as pltpu
from jax.sharding import PartitionSpec as P

MESH = pl.DeviceIdType.MESH
F32 = jnp.float32
BF16 = jnp.bfloat16
EPS = 0.01
LANE = 128
NB = 8
SLOTS = 64
VD = 6
MEM = 16
CH = VD * NB
ROWS = MEM * CH
GROUPS = 3
GV = VD // GROUPS
GC = GV * NB
GR = MEM * GC
GA = GR + GC
HAVE = GV * (MEM + 1)
PAD = 48
EDGE = 7
TILE = 512
NT = (((1,), (1,)), ((), ()))
ORDER, FLAG, LAST, VALID = 0, 1, 2, 3


def slot_place(bi, i):
    base = (lax.axis_index("grid") - 1) * NB
    return jnp.clip(bi[i // 32, i % 4, (i // 4) % NB] - base, 0, 3 * NB - 1)


def slot_table(bi, posv, tabv):
    def fill(i, _):
        posv[pl.ds(i, 1), :] = jnp.full((1, LANE), slot_place(bi, i), jnp.int32)
        return 0

    lax.fori_loop(0, SLOTS, fill, 0)
    pos = posv[...]
    sub = lax.broadcasted_iota(jnp.int32, (SLOTS, LANE), 0)
    lane = lax.broadcasted_iota(jnp.int32, (SLOTS, LANE), 1)
    total = lambda x: jnp.sum(x, axis=0, keepdims=True)
    across = total(jnp.where(sub == lane, pos, 0))
    key = pos * SLOTS + sub
    before = jnp.where(lane < SLOTS, (across * SLOTS + lane < key).astype(jnp.int32), 0)
    rank = jnp.sum(before, axis=1, keepdims=True)
    here = total(jnp.where(rank == lane, pos, 0))
    previous = total(jnp.where(rank + 1 == lane, pos, 0))
    tabv[ORDER : ORDER + 1, :] = total(jnp.where(rank == lane, sub, 0))
    tabv[FLAG : FLAG + 1, :] = jnp.where(lane[:1] > 0, (here == previous).astype(jnp.int32), 0)
    tabv[LAST : LAST + 1, :] = jnp.maximum(total((pos <= lane).astype(jnp.int32)) - 1, 0)
    tabv[VALID : VALID + 1, :] = jnp.minimum(total((pos == lane).astype(jnp.int32)), 1)


def score_rows(layer, group, v, xs, area, varw, gr, total):
    w = area[...] * varw[group * GV + v]
    row = (layer * GROUPS + group) * GA + v * NB

    def at(m):
        return xs[pl.ds(pl.multiple_of(row + m * GC, 8), 8), :]

    y = at(MEM)
    x = [at(m) for m in range(MEM)]
    spread = [jnp.zeros((8, LANE), F32) for _ in range(MEM)]
    pairs = jnp.zeros((8, LANE), F32)
    for m in range(MEM):
        for n in range(m + 1, MEM):
            d = x[m] - x[n]
            q = d * d + EPS
            r = lax.rsqrt(q)
            u = d * r
            pairs += q * r
            spread[m] += u
            spread[n] -= u
    misses = jnp.zeros((8, LANE), F32)
    for m in range(MEM):
        d = x[m] - y
        q = d * d + EPS
        r = lax.rsqrt(q)
        misses += q * r
        g = w * (d * r - spread[m] * (1.0 / (MEM - 1)))
        gr[pl.ds(pl.multiple_of((layer * GROUPS + group) * GR + m * GC + v * NB, 8), 8), :] = g
    return total + w * (misses * (1.0 / MEM) - pairs * (1.0 / (MEM * (MEM - 1))))


def decoder_kernel(
    bi, bc, varw, lat, w_in, b_in, w_out, b_out, target, area, smoothers, out, loss,
    lat_v, w_v, slope, field, recv, xs, blocks, mf, mb, gr, contrib, runs, ext,
    rimsend, rimrecv, fsend, zrecv, zrim, lmem, lgrid, posv, tabv, tab,
    in_sem, out_sem, load_sem, tab_sem, send_sem, recv_sem, hsend_sem, hrecv_sem, fsend_sem, frecv_sem,
    rsend_sem, rrecv_sem, zsend_sem, zrecv_sem, esend_sem, erecv_sem,
    l1send_sem, l1recv_sem, l2send_sem, l2recv_sem,
):
    me = lax.axis_index("member")
    g = lax.axis_index("grid")
    has_low = g > 0
    has_high = g < MEM - 1
    at_edge = jnp.logical_or(g == EDGE, g == EDGE + 1)
    low_near = jnp.logical_and(has_low, g != EDGE + 1)
    high_near = jnp.logical_and(has_high, g != EDGE)
    across = jnp.where(g == EDGE, EDGE + 1, EDGE)
    barrier = pltpu.get_barrier_semaphore()
    width = w_v.shape[0]
    cut = width // 2

    def remote(src, dst, send, recv_, member, grid):
        return pltpu.make_async_remote_copy(
            src_ref=src, dst_ref=dst, send_sem=send, recv_sem=recv_,
            device_id=(member, grid), device_id_type=MESH,
        )

    def greet(i, _):
        peer = lax.rem(me + i, MEM)
        pl.semaphore_signal(barrier, inc=1, device_id=(peer, g), device_id_type=MESH)
        there = lax.rem(g + i, MEM)
        pl.semaphore_signal(barrier, inc=1, device_id=(me, there), device_id_type=MESH)

        @pl.when(at_edge)
        def _():
            pl.semaphore_signal(barrier, inc=1, device_id=(peer, across), device_id_type=MESH)

        return 0

    loads = []
    for n in range(2):
        loads.append((
            pltpu.make_async_copy(
                lat.at[pl.ds(n * TILE, TILE), :], lat_v.at[pl.ds(n * TILE, TILE), :], in_sem.at[2 * n]
            ),
            pltpu.make_async_copy(
                w_in.at[:, pl.ds(n * cut, cut)], w_v.at[:, pl.ds(n * cut, cut)], in_sem.at[2 * n + 1]
            ),
        ))
    for pair in loads:
        for copy in pair:
            copy.start()
    load = pltpu.make_async_copy(smoothers, mf, load_sem)
    load.start()
    lax.fori_loop(1, MEM, greet, 0)

    for b in range(NB):
        ext[pl.ds(b, VD, stride=NB), :] = target[:, b * LANE : (b + 1) * LANE]
    for q in range(GROUPS):
        truth = ext[q * GC : (q + 1) * GC, :]
        xs[q * GA + GR : (q + 1) * GA, :] = truth
        recv[1, q, MEM] = truth.astype(BF16)

    @pl.when(jnp.logical_not(has_low))
    def _():
        recv[0] = jnp.zeros(recv.shape[1:], BF16)

    @pl.when(jnp.logical_not(has_high))
    def _():
        recv[2] = jnp.zeros(recv.shape[1:], BF16)

    @pl.when(jnp.logical_not(low_near))
    def _():
        rimrecv[0] = jnp.zeros(rimrecv.shape[1:], BF16)

    @pl.when(jnp.logical_not(high_near))
    def _():
        rimrecv[1] = jnp.zeros(rimrecv.shape[1:], BF16)

    c = 0.7978845608028654
    a = 0.044715
    for copy in loads[0] + (loads[1][1],):
        copy.wait()

    def forward(i, _):
        @pl.when(i == 1)
        def _():
            loads[1][0].wait()

        rows = pl.ds(pl.multiple_of(i * TILE, TILE), TILE)
        pred = jnp.zeros((TILE, w_out.shape[0]), F32)
        for n in range(0, width, cut):
            z = jnp.dot(lat_v[rows, :], w_v[:, n : n + cut], preferred_element_type=F32)
            z = z + b_in[:, n : n + cut]
            zz = z * z
            t = jnp.tanh(z * (c + (c * a) * zz))
            half = 0.5 + 0.5 * t
            hidden = (z * half).astype(BF16)
            d = half + (0.5 * z) * (1.0 - t * t) * (c + (3.0 * c * a) * zz)
            slope[rows, n : n + cut] = d.astype(BF16)
            pred += lax.dot_general(hidden, w_out[:, n : n + cut], NT, preferred_element_type=F32)
        flipped = (pred + b_out[...]).T
        for b in range(TILE // LANE):
            ext[pl.ds(i * (TILE // LANE) + b, 96, stride=NB), :] = (
                flipped[:, b * LANE : (b + 1) * LANE]
            )
        return 0

    lax.fori_loop(0, width // TILE, forward, 0)
    field[...] = ext[0:ROWS, :].reshape(MEM, GROUPS, GC, LANE).astype(BF16)

    pl.semaphore_wait(barrier, 2 * (MEM - 1) + jnp.where(at_edge, MEM - 1, 0))

    def to_member(q, i):
        peer = lax.rem(me + i, MEM)
        return remote(
            field.at[peer, q], recv.at[1, q, me], send_sem.at[q, i], recv_sem.at[q, i], peer, g
        )

    def halo(q, up):
        side, there = (0, g + 1) if up else (1, g - 1)
        return remote(
            recv.at[1, q], recv.at[0 if up else 2, q],
            hsend_sem.at[side, q], hrecv_sem.at[side, q], me, there,
        )

    def far_truth(q, up):
        side, there = (0, g + 1) if up else (1, g - 1)
        return remote(
            recv.at[1, q, MEM], recv.at[0 if up else 2, q, MEM],
            hsend_sem.at[side, q], hrecv_sem.at[side, q], me, there,
        )

    def far(q, i, up):
        peer = lax.rem(me + i, MEM)
        return remote(
            field.at[peer, q], recv.at[0 if up else 2, q, me],
            fsend_sem.at[q, i], frecv_sem.at[q, i], peer, across,
        )

    def each(start, stop, f, unroll=False):
        def one(i, _):
            f(i)
            return 0

        lax.fori_loop(start, stop, one, 0, unroll=unroll)

    def far_send(q, i):
        @pl.when(g == EDGE)
        def _():
            far(q, i, True).start()

        @pl.when(g == EDGE + 1)
        def _():
            far(q, i, False).start()

    for q in range(GROUPS):

        def send(i):
            to_member(q, i).start()
            far_send(q, i)

        each(1, MEM, send)
        far_send(q, 0)
        recv[1, q, me] = field[me, q]

        @pl.when(g == EDGE)
        def _():
            far_truth(q, True).start()

        @pl.when(g == EDGE + 1)
        def _():
            far_truth(q, False).start()

    slot_table(bi, posv, tabv)
    tab_copy = pltpu.make_async_copy(tabv, tab, tab_sem)
    tab_copy.start()
    load.wait()

    def weights(i):
        live = (i % 4 < bc[i // 32, (i // 4) % NB]).astype(jnp.int32).astype(F32)
        mb[i] = (mf[i // 32, (i // 4) % NB, i % 4] * live).astype(BF16)

    each(0, SLOTS, weights, unroll=4)
    tab_copy.wait()
    pad = jnp.zeros((PAD - HAVE, LANE), BF16)

    def center(q, total):
        each(1, MEM, lambda i: to_member(q, i).wait_recv())

        @pl.when(high_near)
        def _():
            halo(q, True).start()

        @pl.when(low_near)
        def _():
            halo(q, False).start()

        xs[q * GA : q * GA + GR, :] = recv[1, q, 0:MEM].reshape(GR, LANE).astype(F32)
        for b in range(NB):
            blocks[q, NB + b] = jnp.concatenate(
                [xs[pl.ds(q * GA + b, HAVE, stride=NB), :].astype(BF16), pad], axis=0
            )
        return lax.fori_loop(
            0, GV, lambda v, t: score_rows(0, q, v, xs, area, varw, gr, t), total
        )

    def smoothed(q, total):
        @pl.when(low_near)
        def _():
            halo(q, True).wait_recv()

        @pl.when(high_near)
        def _():
            halo(q, False).wait_recv()

        @pl.when(at_edge)
        def _():
            each(0, MEM, lambda i: far(q, i, True).wait_recv())

        @pl.when(g == EDGE)
        def _():
            far_truth(q, False).wait_recv()

        @pl.when(g == EDGE + 1)
        def _():
            far_truth(q, True).wait_recv()

        for side, first in ((0, 0), (2, 2 * NB)):
            ext[0:GA, :] = recv[side, q].reshape(GA, LANE).astype(F32)
            for b in range(NB):
                blocks[q, first + b] = jnp.concatenate(
                    [ext[pl.ds(b, HAVE, stride=NB), :].astype(BF16), pad], axis=0
                )
        for s in range(2):
            for r in range(NB):
                i = (s * NB + r) * 4
                picked = jnp.concatenate(
                    [blocks[q, slot_place(bi, i + k)] for k in range(4)], axis=1
                )
                res = jnp.dot(
                    picked, mb[i : i + 4].reshape(4 * LANE, LANE), preferred_element_type=F32
                )
                row = ((s + 1) * GROUPS + q) * GA + r
                xs[pl.ds(row, HAVE, stride=NB), :] = res[:HAVE]

        def later(i, t):
            return score_rows(1 + i // GV, q, i % GV, xs, area, varw, gr, t)

        return lax.fori_loop(0, 2 * GV, later, total)

    def rim(q, up):
        side, there = (0, g + 1) if up else (1, g - 1)
        return remote(
            rimsend.at[side, q], rimrecv.at[side, q],
            rsend_sem.at[side, q], rrecv_sem.at[side, q], me, there,
        )

    def far_rim(q, i, side):
        peer = lax.rem(me + i, MEM)
        return remote(
            rimsend.at[side, q, peer], zrim.at[me, q],
            esend_sem.at[q, i], erecv_sem.at[q, i], peer, across,
        )

    def adjoint(q):
        for s in range(2):
            for r in range(NB):
                i = (s * NB + r) * 4
                row = ((s + 1) * GROUPS + q) * GR + r
                rows = gr[pl.ds(row, GV * MEM, stride=NB), :].astype(BF16)
                res = lax.dot_general(
                    rows, mb[i : i + 4].reshape(4 * LANE, LANE), NT, preferred_element_type=F32
                )
                for k in range(4):
                    contrib[i + k] = res[:, k * LANE : (k + 1) * LANE]

        def run(t, acc):
            acc = acc * tab[FLAG, t].astype(F32) + contrib[tab[ORDER, t]]
            runs[t] = acc
            return acc

        lax.fori_loop(0, SLOTS, run, jnp.zeros((GV * MEM, LANE), F32), unroll=8)

        def spread(first):
            for p in range(first, first + NB):
                e = runs[tab[LAST, p]] * tab[VALID, p].astype(F32)
                ext[pl.ds(p % NB, GV * MEM, stride=NB), :] = e
            return ext[0:GR, :]

        rimsend[1, q] = spread(0).reshape(MEM, GC, LANE).astype(BF16)

        @pl.when(low_near)
        def _():
            rim(q, False).start()

        @pl.when(g == EDGE + 1)
        def _():
            each(0, MEM, lambda i: far_rim(q, i, 1).start())

        rimsend[0, q] = spread(2 * NB).reshape(MEM, GC, LANE).astype(BF16)

        @pl.when(high_near)
        def _():
            rim(q, True).start()

        @pl.when(g == EDGE)
        def _():
            each(0, MEM, lambda i: far_rim(q, i, 0).start())

        gr[q * GR : (q + 1) * GR, :] += spread(NB)

    def to_owner(q, i):
        peer = lax.rem(me + i, MEM)
        return remote(
            fsend.at[q, peer], zrecv.at[me, q], zsend_sem.at[q, i], zrecv_sem.at[q, i], peer, g
        )

    def give_back(q):
        @pl.when(low_near)
        def _():
            rim(q, True).wait_recv()

        @pl.when(high_near)
        def _():
            rim(q, False).wait_recv()

        value = gr[q * GR : (q + 1) * GR, :]
        value = value + rimrecv[0, q].reshape(GR, LANE).astype(F32)
        value = value + rimrecv[1, q].reshape(GR, LANE).astype(F32)
        fsend[q] = value.reshape(MEM, GC, LANE).astype(BF16)
        each(1, MEM, lambda i: to_owner(q, i).start())
        zrecv[me, q] = fsend[q, me]

    def loss_member(i):
        peer = lax.rem(me + i, MEM)
        return remote(lmem.at[me], lmem.at[me], l1send_sem.at[i], l1recv_sem.at[i], peer, g)

    def loss_grid(i):
        there = lax.rem(g + i, MEM)
        return remote(lgrid.at[g], lgrid.at[g], l2send_sem.at[i], l2recv_sem.at[i], me, there)

    partial = center(0, jnp.zeros((8, LANE), F32))
    partial = center(1, partial)
    partial = smoothed(0, partial)
    adjoint(0)
    partial = center(2, partial)
    partial = smoothed(1, partial)
    adjoint(1)
    give_back(0)
    lmem[me] = smoothed(2, partial)
    adjoint(2)
    each(1, MEM, lambda i: loss_member(i).start())
    give_back(1)
    each(1, MEM, lambda i: loss_member(i).wait_recv())
    lgrid[g] = jnp.sum(lmem[...], axis=0)
    give_back(2)
    each(1, MEM, lambda i: loss_grid(i).start())
    for q in range(GROUPS):
        each(1, MEM, lambda i: to_owner(q, i).wait_recv())
    ext[0:ROWS, :] = zrecv[...].reshape(ROWS, LANE).astype(F32)

    @pl.when(at_edge)
    def _():
        for q in range(GROUPS):
            each(0, MEM, lambda i: far_rim(q, i, 0).wait_recv())
        ext[0:ROWS, :] += zrim[...].reshape(ROWS, LANE).astype(F32)

    stores = [
        pltpu.make_async_copy(
            lat_v.at[pl.ds(n * TILE, TILE), :], out.at[pl.ds(n * TILE, TILE), :], out_sem.at[n]
        )
        for n in range(2)
    ]

    def backward(i, _):
        rows = pl.ds(pl.multiple_of(i * TILE, TILE), TILE)
        parts = []
        for b in range(TILE // LANE):
            parts.append(ext[pl.ds(i * (TILE // LANE) + b, 96, stride=NB), :].T.astype(BF16))
        grad = jnp.concatenate(parts, axis=0)
        pre = []
        for n in range(0, width, cut):
            h = jnp.dot(grad, w_out[:, n : n + cut], preferred_element_type=F32)
            pre.append((h * slope[rows, n : n + cut].astype(F32)).astype(BF16))
        pre = jnp.concatenate(pre, axis=1)
        lat_v[rows, :] = lax.dot_general(pre, w_v[...], NT, preferred_element_type=F32).astype(BF16)
        for n in range(2):

            @pl.when(i == n)
            def _():
                stores[n].start()

        return 0

    lax.fori_loop(0, 2, backward, 0)

    def rest(i):
        loss_grid(i).wait_recv()
        loss_member(i).wait_send()
        loss_grid(i).wait_send()
        for q in range(GROUPS):
            to_member(q, i).wait_send()
            to_owner(q, i).wait_send()

    each(1, MEM, rest)
    points = lat_v.shape[0]
    loss[0, 0] = jnp.sum(jnp.sum(lgrid[...], axis=0)) * (1.0 / (3 * 96 * points * MEM))
    for q in range(GROUPS):

        @pl.when(high_near)
        def _():
            halo(q, True).wait_send()
            rim(q, True).wait_send()

        @pl.when(low_near)
        def _():
            halo(q, False).wait_send()
            rim(q, False).wait_send()

        @pl.when(at_edge)
        def _():
            def one(i):
                far(q, i, True).wait_send()
                far_rim(q, i, 0).wait_send()

            each(0, MEM, one)

        @pl.when(g == EDGE)
        def _():
            far_truth(q, True).wait_send()

        @pl.when(g == EDGE + 1)
        def _():
            far_truth(q, False).wait_send()

    for copy in stores:
        copy.wait()


def on_device(latents, w_in, b_in, w_out, b_out, target, area_weight, var_weight,
              smoothers, block_index, block_count):
    points = latents.shape[1]
    lat = latents.reshape(points, -1)
    width = w_in.shape[1]
    smem = pl.BlockSpec(memory_space=pltpu.SMEM)
    vmem = pl.BlockSpec(memory_space=pltpu.VMEM)
    anywhere = pl.BlockSpec(memory_space=pl.ANY)
    dma = pltpu.SemaphoreType.DMA
    few = dma((GROUPS, MEM))
    some = dma((MEM,))
    grad, loss = pl.pallas_call(
        decoder_kernel,
        out_shape=(
            jax.ShapeDtypeStruct(lat.shape, BF16),
            jax.ShapeDtypeStruct((1, 1), F32),
        ),
        in_specs=[smem, smem, smem, anywhere, anywhere, vmem, vmem, vmem, vmem, vmem, anywhere],
        out_specs=(anywhere, smem),
        scratch_shapes=[
            pltpu.VMEM(lat.shape, BF16),
            pltpu.VMEM(w_in.shape, BF16),
            pltpu.VMEM((points, width), BF16),
            pltpu.VMEM((MEM, GROUPS, GC, LANE), BF16),
            pltpu.VMEM((3, GROUPS, MEM + 1, GC, LANE), BF16),
            pltpu.VMEM((3 * GROUPS * GA, LANE), F32),
            pltpu.VMEM((GROUPS, 3 * NB, PAD, LANE), BF16),
            pltpu.VMEM(smoothers.shape, F32),
            pltpu.VMEM((SLOTS, LANE, LANE), BF16),
            pltpu.VMEM((3 * GROUPS * GR, LANE), F32),
            pltpu.VMEM((SLOTS, GV * MEM, LANE), F32),
            pltpu.VMEM((SLOTS, GV * MEM, LANE), F32),
            pltpu.VMEM((ROWS, LANE), F32),
            pltpu.VMEM((2, GROUPS, MEM, GC, LANE), BF16),
            pltpu.VMEM((2, GROUPS, MEM, GC, LANE), BF16),
            pltpu.VMEM((GROUPS, MEM, GC, LANE), BF16),
            pltpu.VMEM((MEM, GROUPS, GC, LANE), BF16),
            pltpu.VMEM((MEM, GROUPS, GC, LANE), BF16),
            pltpu.VMEM((MEM, 8, LANE), F32),
            pltpu.VMEM((MEM, 8, LANE), F32),
            pltpu.VMEM((SLOTS, LANE), jnp.int32),
            pltpu.VMEM((8, LANE), jnp.int32),
            pltpu.SMEM((8, LANE), jnp.int32),
            dma((4,)), dma((2,)), dma, dma, few, few,
            dma((2, GROUPS)), dma((2, GROUPS)), few, few, dma((2, GROUPS)), dma((2, GROUPS)),
            few, few, few, few, some, some, some, some,
        ],
        compiler_params=pltpu.CompilerParams(
            collective_id=0, has_side_effects=True, vmem_limit_bytes=60 * 1024 * 1024
        ),
    )(
        jnp.transpose(block_index, (0, 2, 1)), block_count, var_weight, lat, w_in,
        b_in.reshape(1, -1), w_out.T, b_out.reshape(1, -1), target,
        area_weight.reshape(NB, LANE), smoothers,
    )
    return grad.reshape(latents.shape), loss.reshape(())


def solution(mesh):
    in_specs = (
        P("member", "grid", None), P(), P(), P(), P(),
        P("member", "grid"), P("grid"), P("member"),
        P(None, "grid", None, None, None), P(None, "grid", None), P(None, "grid"),
    )
    return jax.shard_map(
        on_device, mesh=mesh, in_specs=in_specs,
        out_specs=(P("member", "grid", None), P()), check_vma=False,
    )
```

```python
import functools

import jax
import jax.numpy as jnp
from jax import lax
from jax.experimental import pallas as pl
from jax.experimental.pallas import tpu as pltpu
from jax.sharding import PartitionSpec as P

MESH = pl.DeviceIdType.MESH
F32 = jnp.float32
BF16 = jnp.bfloat16
EPS = 0.01
LANE = 128
NB = 8
SLOTS = 64
VD = 6
MEM = 16
CH = VD * NB
ROWS = MEM * CH
ALL = ROWS + CH
PAD = 112
EDGE = 7
TILE = 512
NT = (((1,), (1,)), ((), ()))
ORDER, FLAG, LAST, VALID = 0, 1, 2, 3


def slot_place(bi, i):
    base = (lax.axis_index("grid") - 1) * NB
    return jnp.clip(bi[i // 32, i % 4, (i // 4) % NB] - base, 0, 3 * NB - 1)


def slot_table(bi, posv, tabv):
    def fill(i, _):
        posv[pl.ds(i, 1), :] = jnp.full((1, LANE), slot_place(bi, i), jnp.int32)
        return 0

    lax.fori_loop(0, SLOTS, fill, 0)
    pos = posv[...]
    sub = lax.broadcasted_iota(jnp.int32, (SLOTS, LANE), 0)
    lane = lax.broadcasted_iota(jnp.int32, (SLOTS, LANE), 1)
    total = lambda x: jnp.sum(x, axis=0, keepdims=True)
    across = total(jnp.where(sub == lane, pos, 0))
    key = pos * SLOTS + sub
    before = jnp.where(lane < SLOTS, (across * SLOTS + lane < key).astype(jnp.int32), 0)
    rank = jnp.sum(before, axis=1, keepdims=True)
    here = total(jnp.where(rank == lane, pos, 0))
    previous = total(jnp.where(rank + 1 == lane, pos, 0))
    tabv[ORDER : ORDER + 1, :] = total(jnp.where(rank == lane, sub, 0))
    tabv[FLAG : FLAG + 1, :] = jnp.where(lane[:1] > 0, (here == previous).astype(jnp.int32), 0)
    tabv[LAST : LAST + 1, :] = jnp.maximum(total((pos <= lane).astype(jnp.int32)) - 1, 0)
    tabv[VALID : VALID + 1, :] = jnp.minimum(total((pos == lane).astype(jnp.int32)), 1)


def score_rows(layer, v, xs, area, varw, gr, total):
    w = area[...] * varw[v]
    row = layer * ALL + v * NB

    def at(m):
        return xs[pl.ds(pl.multiple_of(row + m * CH, 8), 8), :]

    y = at(MEM)
    x = [at(m) for m in range(MEM)]
    spread = [jnp.zeros((8, LANE), F32) for _ in range(MEM)]
    pairs = jnp.zeros((8, LANE), F32)
    for m in range(MEM):
        for n in range(m + 1, MEM):
            d = x[m] - x[n]
            q = d * d + EPS
            r = lax.rsqrt(q)
            u = d * r
            pairs += q * r
            spread[m] += u
            spread[n] -= u
    misses = jnp.zeros((8, LANE), F32)
    for m in range(MEM):
        d = x[m] - y
        q = d * d + EPS
        r = lax.rsqrt(q)
        misses += q * r
        g = w * (d * r - spread[m] * (1.0 / (MEM - 1)))
        gr[pl.ds(pl.multiple_of(layer * ROWS + m * CH + v * NB, 8), 8), :] = g
    return total + w * (misses * (1.0 / MEM) - pairs * (1.0 / (MEM * (MEM - 1))))


def decoder_kernel(
    bi_h, bc_h, varw_h, lat, w_in, b_in_h, w_out_h, b_out_h, target_h, area_h, smoothers, out, loss,
    bi, bc, varw, b_in, w_out, b_out, target, area, small_sem, lsum,
    lat_v, w_v, pre, slope, field, recv, xs, blocks, mf, mb, gr, contrib, runs, ext,
    rimsend, rimrecv, fsend, zrecv, zrim, posv, tabv, tab,
    in_sem, out_sem, load_sem, tab_sem, send_sem, recv_sem, hsend_sem, hrecv_sem,
    rsend_sem, rrecv_sem, zsend_sem, zrecv_sem, esend_sem, erecv_sem,
    lsend_sem, lrecv_sem,
):
    me = lax.axis_index("member")
    g = lax.axis_index("grid")
    has_low = g > 0
    has_high = g < MEM - 1
    at_edge = jnp.logical_or(g == EDGE, g == EDGE + 1)
    low_near = jnp.logical_and(has_low, g != EDGE + 1)
    high_near = jnp.logical_and(has_high, g != EDGE)
    across = jnp.where(g == EDGE, EDGE + 1, EDGE)
    barrier = pltpu.get_barrier_semaphore()
    width = w_v.shape[0]
    cut = width // 2

    def remote(src, dst, send, recv_, member, grid):
        return pltpu.make_async_remote_copy(
            src_ref=src, dst_ref=dst, send_sem=send, recv_sem=recv_,
            device_id=(member, grid), device_id_type=MESH,
        )

    def greet(i, _):
        peer = lax.rem(me + i, MEM)
        pl.semaphore_signal(barrier, inc=1, device_id=(peer, g), device_id_type=MESH)
        @pl.when(at_edge)
        def _():
            pl.semaphore_signal(barrier, inc=1, device_id=(peer, across), device_id_type=MESH)

        return 0

    def quad(stage, i):
        if stage == 0:
            return (me // 4) * 4 + lax.rem(me % 4 + i, 4), g
        if stage == 1:
            return lax.rem(me + 4 * i, MEM), g
        if stage == 2:
            return me, (g // 4) * 4 + lax.rem(g % 4 + i, 4)
        return me, lax.rem(g + 4 * i, MEM)

    small = [
        pltpu.make_async_copy(src, dst, small_sem.at[n])
        for n, (src, dst) in enumerate([
            (w_out_h, w_out), (b_in_h, b_in), (b_out_h, b_out), (target_h, target),
            (area_h, area), (varw_h, varw), (bi_h, bi), (bc_h, bc),
        ])
    ]
    loads = []
    for n in range(2):
        loads.append((
            pltpu.make_async_copy(
                lat.at[pl.ds(n * TILE, TILE), :], lat_v.at[pl.ds(n * TILE, TILE), :], in_sem.at[2 * n]
            ),
            pltpu.make_async_copy(
                w_in.at[:, pl.ds(n * cut, cut)], w_v.at[:, pl.ds(n * cut, cut)], in_sem.at[2 * n + 1]
            ),
        ))
    for copy in (loads[0][0], loads[0][1], loads[1][1], *small, loads[1][0]):
        copy.start()
    load = pltpu.make_async_copy(smoothers, mf, load_sem)
    lax.fori_loop(1, MEM, greet, 0)

    @pl.when(has_low)
    def _():
        pl.semaphore_signal(barrier, inc=1, device_id=(me, g - 1), device_id_type=MESH)

    @pl.when(has_high)
    def _():
        pl.semaphore_signal(barrier, inc=1, device_id=(me, g + 1), device_id_type=MESH)

    for stage in (2, 3):
        for i in range(1, 4):
            pl.semaphore_signal(
                barrier, inc=1, device_id=quad(stage, i), device_id_type=MESH
            )

    @pl.when(jnp.logical_not(has_low))
    def _():
        recv[0] = jnp.zeros(recv.shape[1:], BF16)

    @pl.when(jnp.logical_not(has_high))
    def _():
        recv[2] = jnp.zeros(recv.shape[1:], BF16)

    @pl.when(jnp.logical_not(low_near))
    def _():
        rimrecv[0] = jnp.zeros(rimrecv.shape[1:], BF16)

    @pl.when(jnp.logical_not(high_near))
    def _():
        rimrecv[1] = jnp.zeros(rimrecv.shape[1:], BF16)

    c = 0.7978845608028654
    a = 0.044715
    for copy in small:
        copy.wait()
    for b in range(NB):
        xs[pl.ds(ROWS + b, VD, stride=NB), :] = target[:, b * LANE : (b + 1) * LANE]
    recv[1, MEM] = xs[ROWS:ALL, :].astype(BF16)

    rows96 = lax.broadcasted_iota(jnp.int32, (96, 96), 0)
    cols96 = lax.broadcasted_iota(jnp.int32, (96, 96), 1)
    shift = jnp.sum(jnp.where(rows96 == cols96, b_out[...], 0.0), axis=1, keepdims=True)
    for copy in loads[0] + (loads[1][1],):
        copy.wait()

    def forward(i, _):
        @pl.when(i == 1)
        def _():
            loads[1][0].wait()
            load.start()

        rows = pl.ds(pl.multiple_of(i * TILE, TILE), TILE)
        pred = jnp.broadcast_to(shift, (w_out.shape[0], TILE))
        for n in range(0, width, cut):
            z = jnp.dot(lat_v[rows, :], w_v[:, n : n + cut], preferred_element_type=F32)
            z = z + b_in[:, n : n + cut]
            pre[rows, n : n + cut] = z
            hidden = (z * (0.5 + 0.5 * jnp.tanh(z * (c + (c * a) * (z * z))))).astype(BF16)
            pred += lax.dot_general(w_out[:, n : n + cut], hidden, NT, preferred_element_type=F32)
        for b in range(TILE // LANE):
            ext[pl.ds(i * (TILE // LANE) + b, 96, stride=NB), :] = (
                pred[:, b * LANE : (b + 1) * LANE]
            )
        return 0

    def slopes(first, last):
        def one(i, _):
            rows = pl.ds(pl.multiple_of(i * 128, 128), 128)
            z = pre[rows, :]
            zz = z * z
            t = jnp.tanh(z * (c + (c * a) * zz))
            d = 0.5 + 0.5 * t + (0.5 * z) * (1.0 - t * t) * (c + (3.0 * c * a) * zz)
            slope[rows, :] = d.astype(BF16)
            return 0

        lax.fori_loop(first, last, one, 0)

    lax.fori_loop(0, width // TILE, forward, 0)
    field[...] = ext[0:ROWS, :].reshape(MEM, CH, LANE).astype(BF16)

    pl.semaphore_wait(
        barrier,
        MEM - 1 + 6 + has_low.astype(jnp.int32) + has_high.astype(jnp.int32)
        + jnp.where(at_edge, MEM - 1, 0),
    )

    def to_member(i):
        peer = lax.rem(me + i, MEM)
        return remote(field.at[peer], recv.at[1, me], send_sem.at[i], recv_sem.at[i], peer, g)

    def from_member(i):
        src = lax.rem(me + MEM - i, MEM)
        return remote(field.at[src], recv.at[1, src], send_sem.at[i], recv_sem.at[i], src, g)

    def halo(i, chunk, up):
        side, there = (0, g + 1) if up else (1, g - 1)
        return remote(
            recv.at[1, chunk], recv.at[0 if up else 2, chunk],
            hsend_sem.at[side, i], hrecv_sem.at[side, i], me, there,
        )

    def far(i, up):
        side = 0 if up else 1
        peer = lax.rem(me + i, MEM)
        return remote(
            field.at[peer], recv.at[0 if up else 2, me],
            hsend_sem.at[side, i], hrecv_sem.at[side, i], peer, across,
        )

    def far_send(i):
        @pl.when(g == EDGE)
        def _():
            far(i, True).start()

        @pl.when(g == EDGE + 1)
        def _():
            far(i, False).start()

    def pass_on(i, chunk, up_ok, down_ok):
        @pl.when(up_ok)
        def _():
            halo(i, chunk, True).start()

        @pl.when(down_ok)
        def _():
            halo(i, chunk, False).start()

    def send(i, _):
        to_member(i).start()
        far_send(i)
        return 0

    lax.fori_loop(1, MEM, send, 0)
    far_send(0)
    recv[1, me] = field[me]
    pass_on(MEM, MEM, has_high, has_low)
    pass_on(0, me, high_near, low_near)

    slot_table(bi, posv, tabv)
    tab_copy = pltpu.make_async_copy(tabv, tab, tab_sem)
    tab_copy.start()
    load.wait()

    def weights(i, _):
        live = (i % 4 < bc[i // 32, (i // 4) % NB]).astype(jnp.int32).astype(F32)
        mb[i] = (mf[i // 32, (i // 4) % NB, i % 4] * live).astype(BF16)
        return 0

    lax.fori_loop(0, SLOTS, weights, 0, unroll=4)

    def arrive(i, _):
        from_member(i).wait_recv()
        pass_on(i, lax.rem(me + MEM - i, MEM), high_near, low_near)
        return 0

    lax.fori_loop(1, MEM, arrive, 0)

    xs[0:ROWS, :] = recv[1, 0:MEM].reshape(ROWS, LANE).astype(F32)
    pad = jnp.zeros((PAD - 102, LANE), BF16)
    for b in range(NB):
        blocks[NB + b] = jnp.concatenate(
            [xs[pl.ds(b, 102, stride=NB), :].astype(BF16), pad], axis=0
        )
    partial = lax.fori_loop(
        0, VD, lambda v, t: score_rows(0, v, xs, area, varw, gr, t), jnp.zeros((8, LANE), F32)
    )
    tab_copy.wait()

    def landed(i, _):
        @pl.when(has_low)
        def _():
            halo(i, 0, True).wait_recv()

        @pl.when(has_high)
        def _():
            halo(i, 0, False).wait_recv()

        return 0

    lax.fori_loop(0, MEM + 1, landed, 0)
    for side, first in ((0, 0), (2, 2 * NB)):
        ext[0:ALL, :] = recv[side].reshape(ALL, LANE).astype(F32)
        for b in range(NB):
            blocks[first + b] = jnp.concatenate(
                [ext[pl.ds(b, 102, stride=NB), :].astype(BF16), pad], axis=0
            )

    for s in range(2):
        for r in range(NB):
            i = (s * NB + r) * 4
            picked = jnp.concatenate([blocks[slot_place(bi, i + k)] for k in range(4)], axis=1)
            res = jnp.dot(
                picked, mb[i : i + 4].reshape(4 * LANE, LANE), preferred_element_type=F32
            )
            xs[pl.ds((s + 1) * ALL + r, 102, stride=NB), :] = res[:102]

    def later(i, t):
        return score_rows(1 + i // VD, i % VD, xs, area, varw, gr, t)

    def loss_copy(stage, i):
        mine = (me % 4, me // 4, g % 4, g // 4)[stage]
        return remote(
            lsum.at[stage, mine], lsum.at[stage, mine],
            lsend_sem.at[stage, i], lrecv_sem.at[stage, i], *quad(stage, i),
        )

    def loss_out(stage, value):
        mine = (me % 4, me // 4, g % 4, g // 4)[stage]
        lsum[stage, mine] = value
        for i in range(1, 4):
            loss_copy(stage, i).start()

    def loss_in(stage):
        for i in range(1, 4):
            loss_copy(stage, i).wait_recv()
        return (lsum[stage, 0] + lsum[stage, 1]) + (lsum[stage, 2] + lsum[stage, 3])

    loss_out(0, lax.fori_loop(0, 2 * VD, later, partial))

    for s in range(2):
        for r in range(NB):
            i = (s * NB + r) * 4
            rows = gr[pl.ds((s + 1) * ROWS + r, 96, stride=NB), :].astype(BF16)
            res = lax.dot_general(
                rows, mb[i : i + 4].reshape(4 * LANE, LANE), NT, preferred_element_type=F32
            )
            for k in range(4):
                contrib[i + k] = res[:, k * LANE : (k + 1) * LANE]

    def run(t, acc):
        acc = acc * tab[FLAG, t].astype(F32) + contrib[tab[ORDER, t]]
        runs[t] = acc
        return acc

    lax.fori_loop(0, SLOTS, run, jnp.zeros((96, LANE), F32), unroll=4)

    def spread(first):
        for q in range(first, first + NB):
            e = runs[tab[LAST, q]] * tab[VALID, q].astype(F32)
            ext[pl.ds((q // NB) * ROWS + q % NB, 96, stride=NB), :] = e

    def rim(q, up):
        side, there = (0, g + 1) if up else (1, g - 1)
        some = pl.ds(q * 4, 4)
        return remote(
            rimsend.at[side, some], rimrecv.at[side, some],
            rsend_sem.at[side, q], rrecv_sem.at[side, q], me, there,
        )

    def far_rim(i, side):
        peer = lax.rem(me + i, MEM)
        return remote(
            rimsend.at[side, peer], zrim.at[me], esend_sem.at[i], erecv_sem.at[i], peer, across
        )

    def far_rims(side):
        def one(i, _):
            far_rim(i, side).start()
            return 0

        lax.fori_loop(0, MEM, one, 0)

    spread(0)
    rimsend[1] = ext[0:ROWS, :].reshape(MEM, CH, LANE).astype(BF16)

    @pl.when(low_near)
    def _():
        for q in range(4):
            rim(q, False).start()

    @pl.when(g == EDGE + 1)
    def _():
        far_rims(1)

    spread(2 * NB)
    rimsend[0] = ext[2 * ROWS : 3 * ROWS, :].reshape(MEM, CH, LANE).astype(BF16)

    @pl.when(high_near)
    def _():
        for q in range(4):
            rim(q, True).start()

    @pl.when(g == EDGE)
    def _():
        far_rims(0)

    spread(NB)

    loss_out(1, loss_in(0))
    slopes(0, 8)
    loss_out(2, loss_in(1))

    def to_owner(i):
        peer = lax.rem(me + i, MEM)
        return remote(fsend.at[peer], zrecv.at[me], zsend_sem.at[i], zrecv_sem.at[i], peer, g)

    for q in range(4):

        @pl.when(low_near)
        def _():
            rim(q, True).wait_recv()

        @pl.when(high_near)
        def _():
            rim(q, False).wait_recv()

        for m in range(4 * q, 4 * q + 4):
            at = m * CH
            value = gr[at : at + CH, :] + ext[ROWS + at : ROWS + at + CH, :]
            value = value + (rimrecv[0, m].astype(F32) + rimrecv[1, m].astype(F32))
            fsend[m] = value.astype(BF16)
            i = lax.rem(m - me + MEM, MEM)

            @pl.when(i > 0)
            def _():
                to_owner(i).start()

    zrecv[me] = fsend[me]
    loss_out(3, loss_in(2))

    def owned(i, _):
        src = lax.rem(me + MEM - i, MEM)
        remote(
            fsend.at[src], zrecv.at[src], zsend_sem.at[i], zrecv_sem.at[i], src, g
        ).wait_recv()
        return 0

    lax.fori_loop(1, MEM, owned, 0)
    ext[0:ROWS, :] = zrecv[...].reshape(ROWS, LANE).astype(F32)

    @pl.when(at_edge)
    def _():
        def one(i, _):
            src = lax.rem(me + MEM - i, MEM)
            remote(
                rimsend.at[0, src], zrim.at[src], esend_sem.at[i], erecv_sem.at[i], src, across
            ).wait_recv()
            return 0

        lax.fori_loop(0, MEM, one, 0)
        ext[0:ROWS, :] += zrim[...].reshape(ROWS, LANE).astype(F32)

    stores = [
        pltpu.make_async_copy(
            lat_v.at[pl.ds(n * TILE, TILE), :], out.at[pl.ds(n * TILE, TILE), :], out_sem.at[n]
        )
        for n in range(2)
    ]

    def backward(i, _):
        rows = pl.ds(pl.multiple_of(i * TILE, TILE), TILE)
        grad = jnp.concatenate(
            [
                ext[pl.ds(i * (TILE // LANE) + b, 96, stride=NB), :].astype(BF16)
                for b in range(TILE // LANE)
            ],
            axis=1,
        )
        back = []
        for n in range(0, width, cut):
            h = lax.dot_general(
                grad, w_out[:, n : n + cut], (((0,), (0,)), ((), ())), preferred_element_type=F32
            )
            back.append((h * slope[rows, n : n + cut].astype(F32)).astype(BF16))
        back = jnp.concatenate(back, axis=1)
        lat_v[rows, :] = lax.dot_general(back, w_v[...], NT, preferred_element_type=F32).astype(BF16)
        for n in range(2):

            @pl.when(i == n)
            def _():
                stores[n].start()

        return 0

    lax.fori_loop(0, 2, backward, 0)

    def rest(i, _):
        to_member(i).wait_send()
        to_owner(i).wait_send()
        return 0

    lax.fori_loop(1, MEM, rest, 0)
    points = lat_v.shape[0]
    loss[0, 0] = jnp.sum(loss_in(3)) * (1.0 / (3 * 96 * points * MEM))

    def sent(i, _):
        @pl.when(has_high)
        def _():
            halo(i, 0, True).wait_send()

        @pl.when(has_low)
        def _():
            halo(i, 0, False).wait_send()

        return 0

    lax.fori_loop(0, MEM + 1, sent, 0)

    @pl.when(at_edge)
    def _():
        def one(i, _):
            far_rim(i, 0).wait_send()
            return 0

        lax.fori_loop(0, MEM, one, 0)

    for q in range(4):

        @pl.when(high_near)
        def _():
            rim(q, True).wait_send()

        @pl.when(low_near)
        def _():
            rim(q, False).wait_send()

    for stage in range(4):
        for i in range(1, 4):
            loss_copy(stage, i).wait_send()
    for copy in stores:
        copy.wait()


def on_device(latents, w_in, b_in, w_out, b_out, target, area_weight, var_weight,
              smoothers, block_index, block_count):
    points = latents.shape[1]
    lat = latents.reshape(points, -1)
    width = w_in.shape[1]
    smem = pl.BlockSpec(memory_space=pltpu.SMEM)
    anywhere = pl.BlockSpec(memory_space=pl.ANY)
    dma = pltpu.SemaphoreType.DMA
    some = dma((MEM,))
    chunks = (MEM, CH, LANE)
    grad, loss = pl.pallas_call(
        decoder_kernel,
        out_shape=(
            jax.ShapeDtypeStruct(lat.shape, BF16),
            jax.ShapeDtypeStruct((1, 1), F32),
        ),
        in_specs=[anywhere] * 11,
        out_specs=(anywhere, smem),
        scratch_shapes=[
            pltpu.SMEM((2, 4, NB), jnp.int32),
            pltpu.SMEM((2, NB), jnp.int32),
            pltpu.SMEM((VD,), F32),
            pltpu.VMEM((1, width), F32),
            pltpu.VMEM((96, width), BF16),
            pltpu.VMEM((1, 96), F32),
            pltpu.VMEM((VD, points), F32),
            pltpu.VMEM((NB, LANE), F32),
            dma((8,)),
            pltpu.VMEM((4, 4, 8, LANE), F32),
            pltpu.VMEM(lat.shape, BF16),
            pltpu.VMEM(w_in.shape, BF16),
            pltpu.VMEM((points, width), F32),
            pltpu.VMEM((points, width), BF16),
            pltpu.VMEM(chunks, BF16),
            pltpu.VMEM((3, MEM + 1, CH, LANE), BF16),
            pltpu.VMEM((3 * ALL, LANE), F32),
            pltpu.VMEM((3 * NB, PAD, LANE), BF16),
            pltpu.VMEM(smoothers.shape, F32),
            pltpu.VMEM((SLOTS, LANE, LANE), BF16),
            pltpu.VMEM((3 * ROWS, LANE), F32),
            pltpu.VMEM((SLOTS, 96, LANE), F32),
            pltpu.VMEM((SLOTS, 96, LANE), F32),
            pltpu.VMEM((3 * ROWS, LANE), F32),
            pltpu.VMEM((2,) + chunks, BF16),
            pltpu.VMEM((2,) + chunks, BF16),
            pltpu.VMEM(chunks, BF16),
            pltpu.VMEM(chunks, BF16),
            pltpu.VMEM(chunks, BF16),
            pltpu.VMEM((SLOTS, LANE), jnp.int32),
            pltpu.VMEM((8, LANE), jnp.int32),
            pltpu.SMEM((8, LANE), jnp.int32),
            dma((4,)), dma((2,)), dma, dma, some, some,
            dma((2, MEM + 1)), dma((2, MEM + 1)), dma((2, 4)), dma((2, 4)),
            some, some, some, some, dma((4, 4)), dma((4, 4)),
        ],
        compiler_params=pltpu.CompilerParams(
            collective_id=0, has_side_effects=True, vmem_limit_bytes=60 * 1024 * 1024
        ),
    )(
        jnp.transpose(block_index, (0, 2, 1)), block_count, var_weight, lat, w_in,
        b_in.reshape(1, -1), w_out.T, b_out.reshape(1, -1), target,
        area_weight.reshape(NB, LANE), smoothers,
    )
    return grad.reshape(latents.shape), loss.reshape(())


def solution(mesh):
    in_specs = (
        P("member", "grid", None), P(), P(), P(), P(),
        P("member", "grid"), P("grid"), P("member"),
        P(None, "grid", None, None, None), P(None, "grid", None), P(None, "grid"),
    )
    return jax.shard_map(
        on_device, mesh=mesh, in_specs=in_specs,
        out_specs=(P("member", "grid", None), P()), check_vma=False,
    )
```

```python
import functools

import jax
import jax.numpy as jnp
from jax import lax
from jax.experimental import pallas as pl
from jax.experimental.pallas import tpu as pltpu
from jax.sharding import PartitionSpec as P

MESH = pl.DeviceIdType.MESH
F32 = jnp.float32
BF16 = jnp.bfloat16
EPS = 0.01
LANE = 128
NB = 8
SLOTS = 64
VD = 6
MEM = 16
CH = VD * NB
ROWS = MEM * CH
ALL = ROWS + CH
PAD = 112
EDGE = 7
TILE = 512
NT = (((1,), (1,)), ((), ()))
ORDER, FLAG, LAST, VALID = 0, 1, 2, 3


def slot_place(bi, i):
    base = (lax.axis_index("grid") - 1) * NB
    return jnp.clip(bi[i // 32, i % 4, (i // 4) % NB] - base, 0, 3 * NB - 1)


def slot_table(bi, posv, tabv):
    def fill(i, _):
        posv[pl.ds(i, 1), :] = jnp.full((1, LANE), slot_place(bi, i), jnp.int32)
        return 0

    lax.fori_loop(0, SLOTS, fill, 0)
    pos = posv[...]
    sub = lax.broadcasted_iota(jnp.int32, (SLOTS, LANE), 0)
    lane = lax.broadcasted_iota(jnp.int32, (SLOTS, LANE), 1)
    total = lambda x: jnp.sum(x, axis=0, keepdims=True)
    across = total(jnp.where(sub == lane, pos, 0))
    key = pos * SLOTS + sub
    before = jnp.where(lane < SLOTS, (across * SLOTS + lane < key).astype(jnp.int32), 0)
    rank = jnp.sum(before, axis=1, keepdims=True)
    here = total(jnp.where(rank == lane, pos, 0))
    previous = total(jnp.where(rank + 1 == lane, pos, 0))
    tabv[ORDER : ORDER + 1, :] = total(jnp.where(rank == lane, sub, 0))
    tabv[FLAG : FLAG + 1, :] = jnp.where(lane[:1] > 0, (here == previous).astype(jnp.int32), 0)
    tabv[LAST : LAST + 1, :] = jnp.maximum(total((pos <= lane).astype(jnp.int32)) - 1, 0)
    tabv[VALID : VALID + 1, :] = jnp.minimum(total((pos == lane).astype(jnp.int32)), 1)


def score_rows(layer, v, xs, area, varw, gr, total):
    w = area[...] * varw[v]
    row = layer * ALL + v * NB

    def at(m):
        return xs[pl.ds(pl.multiple_of(row + m * CH, 8), 8), :]

    y = at(MEM)
    x = [at(m) for m in range(MEM)]
    spread = [jnp.zeros((8, LANE), F32) for _ in range(MEM)]
    pairs = jnp.zeros((8, LANE), F32)
    for m in range(MEM):
        for n in range(m + 1, MEM):
            d = x[m] - x[n]
            q = d * d + EPS
            r = lax.rsqrt(q)
            u = d * r
            pairs += r
            spread[m] += u
            spread[n] -= u
    misses = jnp.zeros((8, LANE), F32)
    pairs = EPS * pairs
    for m in range(MEM):
        d = x[m] - y
        pairs += d * spread[m]
        q = d * d + EPS
        r = lax.rsqrt(q)
        misses += q * r
        g = w * (d * r - spread[m] * (1.0 / (MEM - 1)))
        gr[pl.ds(pl.multiple_of(layer * ROWS + m * CH + v * NB, 8), 8), :] = g
    return total + w * (misses * (1.0 / MEM) - pairs * (1.0 / (MEM * (MEM - 1))))


def decoder_kernel(
    bi_h, bc_h, varw_h, lat, w_in, b_in_h, w_out_h, b_out_h, target_h, area_h, smoothers, out, loss,
    bi, bc, varw, b_in, w_out, b_out, target, area, small_sem, lsum,
    lat_v, w_v, pre, slope, field, recv, xs, blocks, mf, mb, gr, contrib, runs, ext,
    rimsend, rimrecv, fsend, zrecv, zrim, posv, tabv, tab,
    in_sem, out_sem, load_sem, tab_sem, send_sem, recv_sem, hsend_sem, hrecv_sem,
    rsend_sem, rrecv_sem, zsend_sem, zrecv_sem, esend_sem, erecv_sem,
    lsend_sem, lrecv_sem,
):
    me = lax.axis_index("member")
    g = lax.axis_index("grid")
    has_low = g > 0
    has_high = g < MEM - 1
    at_edge = jnp.logical_or(g == EDGE, g == EDGE + 1)
    low_near = jnp.logical_and(has_low, g != EDGE + 1)
    high_near = jnp.logical_and(has_high, g != EDGE)
    across = jnp.where(g == EDGE, EDGE + 1, EDGE)
    barrier = pltpu.get_barrier_semaphore()
    width = w_v.shape[0]
    cut = width // 2

    def remote(src, dst, send, recv_, member, grid):
        return pltpu.make_async_remote_copy(
            src_ref=src, dst_ref=dst, send_sem=send, recv_sem=recv_,
            device_id=(member, grid), device_id_type=MESH,
        )

    def partner(i, back=False):
        z_lo = me % 4
        kind = i // 4
        z = jnp.where(kind == 1, 3 - z_lo, jnp.where(kind == 2, z_lo + 1 - 2 * (z_lo % 2), z_lo))
        z = jnp.where(kind == 0, (z_lo + 2) % 4, z)
        turn = (i + 1) % 4
        if back:
            turn = 4 - turn
        return ((me // 4 + turn) % 4) * 4 + z

    SELF = MEM - 1

    def greet(i, _):
        peer = partner(i)
        pl.semaphore_signal(barrier, inc=1, device_id=(peer, g), device_id_type=MESH)
        @pl.when(at_edge)
        def _():
            pl.semaphore_signal(barrier, inc=1, device_id=(peer, across), device_id_type=MESH)

        return 0

    def quad(stage, i):
        if stage == 0:
            return (me // 4) * 4 + lax.rem(me % 4 + i, 4), g
        if stage == 1:
            return lax.rem(me + 4 * i, MEM), g
        if stage == 2:
            return me, (g // 4) * 4 + lax.rem(g % 4 + i, 4)
        return me, lax.rem(g + 4 * i, MEM)

    small = [
        pltpu.make_async_copy(src, dst, small_sem.at[n])
        for n, (src, dst) in enumerate([
            (w_out_h, w_out), (b_in_h, b_in), (b_out_h, b_out), (target_h, target),
            (area_h, area), (varw_h, varw), (bi_h, bi), (bc_h, bc),
        ])
    ]
    loads = []
    for n in range(2):
        loads.append((
            pltpu.make_async_copy(
                lat.at[pl.ds(n * TILE, TILE), :], lat_v.at[pl.ds(n * TILE, TILE), :], in_sem.at[2 * n]
            ),
            pltpu.make_async_copy(
                w_in.at[:, pl.ds(n * cut, cut)], w_v.at[:, pl.ds(n * cut, cut)], in_sem.at[2 * n + 1]
            ),
        ))
    for copy in (loads[0][1], loads[0][0], *small, loads[1][1], loads[1][0]):
        copy.start()
    load = pltpu.make_async_copy(smoothers, mf, load_sem)
    lax.fori_loop(0, SELF, greet, 0)

    @pl.when(has_low)
    def _():
        pl.semaphore_signal(barrier, inc=1, device_id=(me, g - 1), device_id_type=MESH)

    @pl.when(has_high)
    def _():
        pl.semaphore_signal(barrier, inc=1, device_id=(me, g + 1), device_id_type=MESH)

    for stage in (2, 3):
        for i in range(1, 4):
            pl.semaphore_signal(
                barrier, inc=1, device_id=quad(stage, i), device_id_type=MESH
            )

    @pl.when(jnp.logical_not(has_low))
    def _():
        recv[0] = jnp.zeros(recv.shape[1:], BF16)

    @pl.when(jnp.logical_not(has_high))
    def _():
        recv[2] = jnp.zeros(recv.shape[1:], BF16)

    @pl.when(jnp.logical_not(low_near))
    def _():
        rimrecv[0] = jnp.zeros(rimrecv.shape[1:], BF16)

    @pl.when(jnp.logical_not(high_near))
    def _():
        rimrecv[1] = jnp.zeros(rimrecv.shape[1:], BF16)

    c = 0.7978845608028654
    a = 0.044715
    for copy in small:
        copy.wait()
    for b in range(NB):
        xs[pl.ds(ROWS + b, VD, stride=NB), :] = target[:, b * LANE : (b + 1) * LANE]
    recv[1, MEM] = xs[ROWS:ALL, :].astype(BF16)

    rows96 = lax.broadcasted_iota(jnp.int32, (96, 96), 0)
    cols96 = lax.broadcasted_iota(jnp.int32, (96, 96), 1)
    shift = jnp.sum(jnp.where(rows96 == cols96, b_out[...], 0.0), axis=1, keepdims=True)
    for copy in loads[0]:
        copy.wait()

    def forward(i, _):
        @pl.when(i == 1)
        def _():
            loads[1][0].wait()

        rows = pl.ds(pl.multiple_of(i * TILE, TILE), TILE)
        pred = jnp.broadcast_to(shift, (w_out.shape[0], TILE))
        for n in range(0, width, cut):
            if n > 0:

                @pl.when(i == 0)
                def _():
                    loads[1][1].wait()
                    load.start()

            z = jnp.dot(lat_v[rows, :], w_v[:, n : n + cut], preferred_element_type=F32)
            z = z + b_in[:, n : n + cut]
            pre[rows, n : n + cut] = z
            hidden = (z * (0.5 + 0.5 * jnp.tanh(z * (c + (c * a) * (z * z))))).astype(BF16)
            pred += lax.dot_general(w_out[:, n : n + cut], hidden, NT, preferred_element_type=F32)
        for b in range(TILE // LANE):
            ext[pl.ds(i * (TILE // LANE) + b, 96, stride=NB), :] = (
                pred[:, b * LANE : (b + 1) * LANE]
            )
        return 0

    def slopes(first, last):
        def one(i, _):
            rows = pl.ds(pl.multiple_of(i * 128, 128), 128)
            z = pre[rows, :]
            zz = z * z
            t = jnp.tanh(z * (c + (c * a) * zz))
            d = 0.5 + 0.5 * t + (0.5 * z) * (1.0 - t * t) * (c + (3.0 * c * a) * zz)
            slope[rows, :] = d.astype(BF16)
            return 0

        lax.fori_loop(first, last, one, 0)

    lax.fori_loop(0, width // TILE, forward, 0)
    field[...] = ext[0:ROWS, :].reshape(MEM, CH, LANE).astype(BF16)

    pl.semaphore_wait(
        barrier,
        MEM - 1 + 6 + has_low.astype(jnp.int32) + has_high.astype(jnp.int32)
        + jnp.where(at_edge, MEM - 1, 0),
    )

    def to_member(i):
        peer = partner(i)
        return remote(field.at[peer], recv.at[1, me], send_sem.at[i], recv_sem.at[i], peer, g)

    def from_member(i):
        src = partner(i, True)
        return remote(field.at[src], recv.at[1, src], send_sem.at[i], recv_sem.at[i], src, g)

    def halo(i, chunk, up):
        side, there = (0, g + 1) if up else (1, g - 1)
        return remote(
            recv.at[1, chunk], recv.at[0 if up else 2, chunk],
            hsend_sem.at[side, i], hrecv_sem.at[side, i], me, there,
        )

    def far(i, up):
        side = 0 if up else 1
        peer = partner(i)
        return remote(
            field.at[peer], recv.at[0 if up else 2, me],
            hsend_sem.at[side, i], hrecv_sem.at[side, i], peer, across,
        )

    def far_send(i):
        @pl.when(g == EDGE)
        def _():
            far(i, True).start()

        @pl.when(g == EDGE + 1)
        def _():
            far(i, False).start()

    def pass_on(i, chunk, up_ok, down_ok):
        @pl.when(up_ok)
        def _():
            halo(i, chunk, True).start()

        @pl.when(down_ok)
        def _():
            halo(i, chunk, False).start()

    def send(i, _):
        to_member(i).start()
        far_send(i)
        return 0

    lax.fori_loop(0, SELF, send, 0)
    far_send(SELF)
    recv[1, me] = field[me]
    pass_on(MEM, MEM, has_high, has_low)
    pass_on(SELF, me, high_near, low_near)

    slot_table(bi, posv, tabv)
    tab_copy = pltpu.make_async_copy(tabv, tab, tab_sem)
    tab_copy.start()
    load.wait()

    def weights(i, _):
        live = (i % 4 < bc[i // 32, (i // 4) % NB]).astype(jnp.int32).astype(F32)
        mb[i] = (mf[i // 32, (i // 4) % NB, i % 4] * live).astype(BF16)
        return 0

    lax.fori_loop(0, SLOTS, weights, 0, unroll=4)

    def arrive(i, _):
        i = SELF - 1 - i
        from_member(i).wait_recv()
        pass_on(i, partner(i, True), high_near, low_near)
        return 0

    lax.fori_loop(0, SELF, arrive, 0)

    xs[0:ROWS, :] = recv[1, 0:MEM].reshape(ROWS, LANE).astype(F32)
    pad = jnp.zeros((PAD - 102, LANE), BF16)
    for b in range(NB):
        blocks[NB + b] = jnp.concatenate(
            [xs[pl.ds(b, 102, stride=NB), :].astype(BF16), pad], axis=0
        )
    partial = lax.fori_loop(
        0, VD, lambda v, t: score_rows(0, v, xs, area, varw, gr, t), jnp.zeros((8, LANE), F32)
    )
    tab_copy.wait()

    def landed(i, _):
        @pl.when(has_low)
        def _():
            halo(i, 0, True).wait_recv()

        @pl.when(has_high)
        def _():
            halo(i, 0, False).wait_recv()

        return 0

    lax.fori_loop(0, MEM + 1, landed, 0)
    for side, first in ((0, 0), (2, 2 * NB)):
        ext[0:ALL, :] = recv[side].reshape(ALL, LANE).astype(F32)
        for b in range(NB):
            blocks[first + b] = jnp.concatenate(
                [ext[pl.ds(b, 102, stride=NB), :].astype(BF16), pad], axis=0
            )

    for s in range(2):
        for r in range(NB):
            i = (s * NB + r) * 4
            picked = jnp.concatenate([blocks[slot_place(bi, i + k)] for k in range(4)], axis=1)
            res = jnp.dot(
                picked, mb[i : i + 4].reshape(4 * LANE, LANE), preferred_element_type=F32
            )
            xs[pl.ds((s + 1) * ALL + r, 102, stride=NB), :] = res[:102]

    def later(i, t):
        return score_rows(1 + i // VD, i % VD, xs, area, varw, gr, t)

    def loss_copy(stage, i):
        mine = (me % 4, me // 4, g % 4, g // 4)[stage]
        return remote(
            lsum.at[stage, mine], lsum.at[stage, mine],
            lsend_sem.at[stage, i], lrecv_sem.at[stage, i], *quad(stage, i),
        )

    def loss_out(stage, value):
        mine = (me % 4, me // 4, g % 4, g // 4)[stage]
        lsum[stage, mine] = value
        for i in range(1, 4):
            loss_copy(stage, i).start()

    def loss_in(stage):
        for i in range(1, 4):
            loss_copy(stage, i).wait_recv()
        return (lsum[stage, 0] + lsum[stage, 1]) + (lsum[stage, 2] + lsum[stage, 3])

    loss_out(0, lax.fori_loop(0, 2 * VD, later, partial))

    for s in range(2):
        for r in range(NB):
            i = (s * NB + r) * 4
            rows = gr[pl.ds((s + 1) * ROWS + r, 96, stride=NB), :].astype(BF16)
            res = lax.dot_general(
                rows, mb[i : i + 4].reshape(4 * LANE, LANE), NT, preferred_element_type=F32
            )
            for k in range(4):
                contrib[i + k] = res[:, k * LANE : (k + 1) * LANE]

    def run(t, acc):
        acc = acc * tab[FLAG, t].astype(F32) + contrib[tab[ORDER, t]]
        runs[t] = acc
        return acc

    lax.fori_loop(0, SLOTS, run, jnp.zeros((96, LANE), F32), unroll=4)

    def spread(first):
        for q in range(first, first + NB):
            e = runs[tab[LAST, q]] * tab[VALID, q].astype(F32)
            ext[pl.ds((q // NB) * ROWS + q % NB, 96, stride=NB), :] = e

    def rim(q, up):
        side, there = (0, g + 1) if up else (1, g - 1)
        some = pl.ds(q * 4, 4)
        return remote(
            rimsend.at[side, some], rimrecv.at[side, some],
            rsend_sem.at[side, q], rrecv_sem.at[side, q], me, there,
        )

    def far_rim(i, side):
        peer = partner(i)
        return remote(
            rimsend.at[side, peer], zrim.at[me], esend_sem.at[i], erecv_sem.at[i], peer, across
        )

    def far_rims(side):
        def one(i, _):
            far_rim(i, side).start()
            return 0

        lax.fori_loop(0, MEM, one, 0)

    spread(0)
    rimsend[1] = ext[0:ROWS, :].reshape(MEM, CH, LANE).astype(BF16)

    @pl.when(low_near)
    def _():
        for q in range(4):
            rim(q, False).start()

    @pl.when(g == EDGE + 1)
    def _():
        far_rims(1)

    spread(2 * NB)
    rimsend[0] = ext[2 * ROWS : 3 * ROWS, :].reshape(MEM, CH, LANE).astype(BF16)

    @pl.when(high_near)
    def _():
        for q in range(4):
            rim(q, True).start()

    @pl.when(g == EDGE)
    def _():
        far_rims(0)

    spread(NB)

    loss_out(1, loss_in(0))
    slopes(0, 8)
    loss_out(2, loss_in(1))

    def to_owner(i):
        peer = partner(i)
        return remote(fsend.at[peer], zrecv.at[me], zsend_sem.at[i], zrecv_sem.at[i], peer, g)

    for q in range(4):

        @pl.when(low_near)
        def _():
            rim(q, True).wait_recv()

        @pl.when(high_near)
        def _():
            rim(q, False).wait_recv()

        at = 4 * q * CH
        value = gr[at : at + 4 * CH, :] + ext[ROWS + at : ROWS + at + 4 * CH, :]
        some = slice(4 * q, 4 * q + 4)
        value = value + rimrecv[0, some].reshape(4 * CH, LANE).astype(F32)
        value = value + rimrecv[1, some].reshape(4 * CH, LANE).astype(F32)
        fsend[some] = value.reshape(4, CH, LANE).astype(BF16)
        turn = (q - me // 4 + 4) % 4
        for kind in range(4):
            i = kind * 4 + (turn + 3) % 4

            @pl.when(i < SELF)
            def _():
                to_owner(i).start()

    zrecv[me] = fsend[me]
    loss_out(3, loss_in(2))

    def owned(i, _):
        src = partner(i, True)
        remote(
            fsend.at[src], zrecv.at[src], zsend_sem.at[i], zrecv_sem.at[i], src, g
        ).wait_recv()
        return 0

    lax.fori_loop(0, SELF, owned, 0)
    ext[0:ROWS, :] = zrecv[...].reshape(ROWS, LANE).astype(F32)

    @pl.when(at_edge)
    def _():
        def one(i, _):
            src = partner(i, True)
            remote(
                rimsend.at[0, src], zrim.at[src], esend_sem.at[i], erecv_sem.at[i], src, across
            ).wait_recv()
            return 0

        lax.fori_loop(0, MEM, one, 0)
        ext[0:ROWS, :] += zrim[...].reshape(ROWS, LANE).astype(F32)

    stores = [
        pltpu.make_async_copy(
            lat_v.at[pl.ds(n * TILE, TILE), :], out.at[pl.ds(n * TILE, TILE), :], out_sem.at[n]
        )
        for n in range(2)
    ]

    def backward(i, _):
        rows = pl.ds(pl.multiple_of(i * TILE, TILE), TILE)
        grad = jnp.concatenate(
            [
                ext[pl.ds(i * (TILE // LANE) + b, 96, stride=NB), :].astype(BF16)
                for b in range(TILE // LANE)
            ],
            axis=1,
        )
        back = []
        for n in range(0, width, cut):
            h = lax.dot_general(
                grad, w_out[:, n : n + cut], (((0,), (0,)), ((), ())), preferred_element_type=F32
            )
            back.append((h * slope[rows, n : n + cut].astype(F32)).astype(BF16))
        back = jnp.concatenate(back, axis=1)
        lat_v[rows, :] = lax.dot_general(back, w_v[...], NT, preferred_element_type=F32).astype(BF16)
        for n in range(2):

            @pl.when(i == n)
            def _():
                stores[n].start()

        return 0

    lax.fori_loop(0, 2, backward, 0)

    def rest(i, _):
        to_member(i).wait_send()
        to_owner(i).wait_send()
        return 0

    lax.fori_loop(0, SELF, rest, 0)
    points = lat_v.shape[0]
    loss[0, 0] = jnp.sum(loss_in(3)) * (1.0 / (3 * 96 * points * MEM))

    def sent(i, _):
        @pl.when(has_high)
        def _():
            halo(i, 0, True).wait_send()

        @pl.when(has_low)
        def _():
            halo(i, 0, False).wait_send()

        return 0

    lax.fori_loop(0, MEM + 1, sent, 0)

    @pl.when(at_edge)
    def _():
        def one(i, _):
            far_rim(i, 0).wait_send()
            return 0

        lax.fori_loop(0, MEM, one, 0)

    for q in range(4):

        @pl.when(high_near)
        def _():
            rim(q, True).wait_send()

        @pl.when(low_near)
        def _():
            rim(q, False).wait_send()

    for stage in range(4):
        for i in range(1, 4):
            loss_copy(stage, i).wait_send()
    for copy in stores:
        copy.wait()


def copy_kernel(x, out, held, in_sem, out_sem):
    count = in_sem.shape[0]
    size = x.shape[0] // count
    some = [pl.ds(n * size, size) for n in range(count)]
    ins = [
        pltpu.make_async_copy(x.at[rows], held.at[rows], in_sem.at[n])
        for n, rows in enumerate(some)
    ]
    outs = [
        pltpu.make_async_copy(held.at[rows], out.at[rows], out_sem.at[n])
        for n, rows in enumerate(some)
    ]
    for copy in ins:
        copy.start()
    for first, second in zip(ins, outs):
        first.wait()
        second.start()
    for copy in outs:
        copy.wait()


def on_device(latents, w_in, b_in, w_out, b_out, target, area_weight, var_weight,
              smoothers, block_index, block_count):
    points = latents.shape[1]
    lat = latents.reshape(points, -1)
    width = w_in.shape[1]
    smem = pl.BlockSpec(memory_space=pltpu.SMEM)
    anywhere = pl.BlockSpec(memory_space=pl.ANY)
    dma = pltpu.SemaphoreType.DMA
    some = dma((MEM,))
    chunks = (MEM, CH, LANE)
    grad, loss = pl.pallas_call(
        decoder_kernel,
        out_shape=(
            jax.ShapeDtypeStruct(lat.shape, BF16),
            jax.ShapeDtypeStruct((1, 1), F32),
        ),
        in_specs=[anywhere] * 11,
        out_specs=(anywhere, smem),
        scratch_shapes=[
            pltpu.SMEM((2, 4, NB), jnp.int32),
            pltpu.SMEM((2, NB), jnp.int32),
            pltpu.SMEM((VD,), F32),
            pltpu.VMEM((1, width), F32),
            pltpu.VMEM((96, width), BF16),
            pltpu.VMEM((1, 96), F32),
            pltpu.VMEM((VD, points), F32),
            pltpu.VMEM((NB, LANE), F32),
            dma((8,)),
            pltpu.VMEM((4, 4, 8, LANE), F32),
            pltpu.VMEM(lat.shape, BF16),
            pltpu.VMEM(w_in.shape, BF16),
            pltpu.VMEM((points, width), F32),
            pltpu.VMEM((points, width), BF16),
            pltpu.VMEM(chunks, BF16),
            pltpu.VMEM((3, MEM + 1, CH, LANE), BF16),
            pltpu.VMEM((3 * ALL, LANE), F32),
            pltpu.VMEM((3 * NB, PAD, LANE), BF16),
            pltpu.VMEM(smoothers.shape, F32),
            pltpu.VMEM((SLOTS, LANE, LANE), BF16),
            pltpu.VMEM((3 * ROWS, LANE), F32),
            pltpu.VMEM((SLOTS, 96, LANE), F32),
            pltpu.VMEM((SLOTS, 96, LANE), F32),
            pltpu.VMEM((3 * ROWS, LANE), F32),
            pltpu.VMEM((2,) + chunks, BF16),
            pltpu.VMEM((2,) + chunks, BF16),
            pltpu.VMEM(chunks, BF16),
            pltpu.VMEM(chunks, BF16),
            pltpu.VMEM(chunks, BF16),
            pltpu.VMEM((SLOTS, LANE), jnp.int32),
            pltpu.VMEM((8, LANE), jnp.int32),
            pltpu.SMEM((8, LANE), jnp.int32),
            dma((4,)), dma((2,)), dma, dma, some, some,
            dma((2, MEM + 1)), dma((2, MEM + 1)), dma((2, 4)), dma((2, 4)),
            some, some, some, some, dma((4, 4)), dma((4, 4)),
        ],
        compiler_params=pltpu.CompilerParams(
            collective_id=0, has_side_effects=True, vmem_limit_bytes=60 * 1024 * 1024
        ),
    )(
        jnp.transpose(block_index, (0, 2, 1)), block_count, var_weight, lat, w_in,
        b_in.reshape(1, -1), w_out.T, b_out.reshape(1, -1), target,
        area_weight.reshape(NB, LANE), smoothers,
    )
    result = pl.pallas_call(
        copy_kernel,
        out_shape=jax.ShapeDtypeStruct(lat.shape, BF16),
        in_specs=[anywhere],
        out_specs=anywhere,
        scratch_shapes=[pltpu.VMEM(lat.shape, BF16), dma((4,)), dma((4,))],
        compiler_params=pltpu.CompilerParams(vmem_limit_bytes=62 * 1024 * 1024),
    )(grad)
    return result.reshape(latents.shape), loss.reshape(())


def solution(mesh):
    in_specs = (
        P("member", "grid", None), P(), P(), P(), P(),
        P("member", "grid"), P("grid"), P("member"),
        P(None, "grid", None, None, None), P(None, "grid", None), P(None, "grid"),
    )
    return jax.shard_map(
        on_device, mesh=mesh, in_specs=in_specs,
        out_specs=(P("member", "grid", None), P()), check_vma=False,
    )
```

```python
import functools

import jax
import jax.numpy as jnp
from jax import lax
from jax.experimental import pallas as pl
from jax.experimental.pallas import tpu as pltpu
from jax.sharding import PartitionSpec as P

MESH = pl.DeviceIdType.MESH
F32 = jnp.float32
BF16 = jnp.bfloat16
EPS = 0.01
LANE = 128
NB = 8
SLOTS = 64
VD = 6
MEM = 16
CH = VD * NB
ROWS = MEM * CH
ALL = ROWS + CH
PAD = 112
EDGE = 7
TILE = 512
NT = (((1,), (1,)), ((), ()))
ORDER, FLAG, LAST, VALID = 0, 1, 2, 3


def slot_place(bi, i):
    base = (lax.axis_index("grid") - 1) * NB
    return jnp.clip(bi[i // 32, i % 4, (i // 4) % NB] - base, 0, 3 * NB - 1)


def slot_table(bi, posv, tabv):
    def fill(i, _):
        posv[pl.ds(i, 1), :] = jnp.full((1, LANE), slot_place(bi, i), jnp.int32)
        return 0

    lax.fori_loop(0, SLOTS, fill, 0)
    pos = posv[...]
    sub = lax.broadcasted_iota(jnp.int32, (SLOTS, LANE), 0)
    lane = lax.broadcasted_iota(jnp.int32, (SLOTS, LANE), 1)
    total = lambda x: jnp.sum(x, axis=0, keepdims=True)
    across = total(jnp.where(sub == lane, pos, 0))
    key = pos * SLOTS + sub
    before = jnp.where(lane < SLOTS, (across * SLOTS + lane < key).astype(jnp.int32), 0)
    rank = jnp.sum(before, axis=1, keepdims=True)
    here = total(jnp.where(rank == lane, pos, 0))
    previous = total(jnp.where(rank + 1 == lane, pos, 0))
    tabv[ORDER : ORDER + 1, :] = total(jnp.where(rank == lane, sub, 0))
    tabv[FLAG : FLAG + 1, :] = jnp.where(lane[:1] > 0, (here == previous).astype(jnp.int32), 0)
    tabv[LAST : LAST + 1, :] = jnp.maximum(total((pos <= lane).astype(jnp.int32)) - 1, 0)
    tabv[VALID : VALID + 1, :] = jnp.minimum(total((pos == lane).astype(jnp.int32)), 1)


def score_rows(layer, v, xs, area, varw, gr, total):
    w = area[...] * varw[v]
    row = layer * ALL + v * NB

    def at(m):
        return xs[pl.ds(pl.multiple_of(row + m * CH, 8), 8), :]

    y = at(MEM)
    x = [at(m) for m in range(MEM)]
    spread = [jnp.zeros((8, LANE), F32) for _ in range(MEM)]
    pairs = jnp.zeros((8, LANE), F32)
    for m in range(MEM):
        for n in range(m + 1, MEM):
            d = x[m] - x[n]
            q = d * d + EPS
            r = lax.rsqrt(q)
            u = d * r
            pairs += r
            spread[m] += u
            spread[n] -= u
    misses = jnp.zeros((8, LANE), F32)
    pairs = EPS * pairs
    for m in range(MEM):
        d = x[m] - y
        pairs += d * spread[m]
        q = d * d + EPS
        r = lax.rsqrt(q)
        misses += q * r
        g = w * (d * r - spread[m] * (1.0 / (MEM - 1)))
        gr[pl.ds(pl.multiple_of(layer * ROWS + m * CH + v * NB, 8), 8), :] = g
    return total + w * (misses * (1.0 / MEM) - pairs * (1.0 / (MEM * (MEM - 1))))


def decoder_kernel(
    bi_h, bc_h, varw_h, lat, w_in, b_in_h, w_out_h, b_out_h, target_h, area_h, smoothers, out, loss,
    bi, bc, varw, b_in, w_out, b_out, target, area, small_sem, lsum,
    lat_v, w_v, pre, slope, field, recv, xs, blocks, mf, mb, gr, contrib, runs, ext,
    rimsend, rimrecv, fsend, zrecv, zrim, posv, tabv, tab,
    in_sem, out_sem, load_sem, tab_sem, send_sem, recv_sem, hsend_sem, hrecv_sem,
    rsend_sem, rrecv_sem, zsend_sem, zrecv_sem, esend_sem, erecv_sem,
    lsend_sem, lrecv_sem,
):
    me = lax.axis_index("member")
    g = lax.axis_index("grid")
    has_low = g > 0
    has_high = g < MEM - 1
    at_edge = jnp.logical_or(g == EDGE, g == EDGE + 1)
    low_near = jnp.logical_and(has_low, g != EDGE + 1)
    high_near = jnp.logical_and(has_high, g != EDGE)
    across = jnp.where(g == EDGE, EDGE + 1, EDGE)
    barrier = pltpu.get_barrier_semaphore()
    width = w_v.shape[0]
    cut = width // 2

    def remote(src, dst, send, recv_, member, grid):
        return pltpu.make_async_remote_copy(
            src_ref=src, dst_ref=dst, send_sem=send, recv_sem=recv_,
            device_id=(member, grid), device_id_type=MESH,
        )

    def partner(i, back=False):
        z_lo = me % 4
        kind = i // 4
        z = jnp.where(kind == 1, 3 - z_lo, jnp.where(kind == 2, z_lo + 1 - 2 * (z_lo % 2), z_lo))
        z = jnp.where(kind == 0, (z_lo + 2) % 4, z)
        turn = (i + 1) % 4
        if back:
            turn = 4 - turn
        return ((me // 4 + turn) % 4) * 4 + z

    SELF = MEM - 1

    def greet(i, _):
        peer = partner(i)
        pl.semaphore_signal(barrier, inc=1, device_id=(peer, g), device_id_type=MESH)
        @pl.when(at_edge)
        def _():
            pl.semaphore_signal(barrier, inc=1, device_id=(peer, across), device_id_type=MESH)

        return 0

    def quad(stage, i):
        if stage == 0:
            return (me // 4) * 4 + lax.rem(me % 4 + i, 4), g
        if stage == 1:
            return lax.rem(me + 4 * i, MEM), g
        if stage == 2:
            return me, (g // 4) * 4 + lax.rem(g % 4 + i, 4)
        return me, lax.rem(g + 4 * i, MEM)

    small = [
        pltpu.make_async_copy(src, dst, small_sem.at[n])
        for n, (src, dst) in enumerate([
            (w_out_h, w_out), (b_in_h, b_in), (b_out_h, b_out), (target_h, target),
            (area_h, area), (varw_h, varw), (bi_h, bi), (bc_h, bc),
        ])
    ]
    loads = []
    for n in range(2):
        loads.append((
            pltpu.make_async_copy(
                lat.at[pl.ds(n * TILE, TILE), :], lat_v.at[pl.ds(n * TILE, TILE), :], in_sem.at[2 * n]
            ),
            pltpu.make_async_copy(
                w_in.at[:, pl.ds(n * cut, cut)], w_v.at[:, pl.ds(n * cut, cut)], in_sem.at[2 * n + 1]
            ),
        ))
    for copy in (loads[0][1], loads[0][0], *small, loads[1][1], loads[1][0]):
        copy.start()
    load = pltpu.make_async_copy(smoothers, mf, load_sem)
    lax.fori_loop(0, SELF, greet, 0)

    @pl.when(has_low)
    def _():
        pl.semaphore_signal(barrier, inc=1, device_id=(me, g - 1), device_id_type=MESH)

    @pl.when(has_high)
    def _():
        pl.semaphore_signal(barrier, inc=1, device_id=(me, g + 1), device_id_type=MESH)

    for stage in (2, 3):
        for i in range(1, 4):
            pl.semaphore_signal(
                barrier, inc=1, device_id=quad(stage, i), device_id_type=MESH
            )

    @pl.when(jnp.logical_not(has_low))
    def _():
        recv[0] = jnp.zeros(recv.shape[1:], BF16)

    @pl.when(jnp.logical_not(has_high))
    def _():
        recv[2] = jnp.zeros(recv.shape[1:], BF16)

    @pl.when(jnp.logical_not(low_near))
    def _():
        rimrecv[0] = jnp.zeros(rimrecv.shape[1:], BF16)

    @pl.when(jnp.logical_not(high_near))
    def _():
        rimrecv[1] = jnp.zeros(rimrecv.shape[1:], BF16)

    c = 0.7978845608028654
    a = 0.044715
    for copy in small:
        copy.wait()
    for b in range(NB):
        xs[pl.ds(ROWS + b, VD, stride=NB), :] = target[:, b * LANE : (b + 1) * LANE]
    recv[1, MEM] = xs[ROWS:ALL, :].astype(BF16)

    rows96 = lax.broadcasted_iota(jnp.int32, (96, 96), 0)
    cols96 = lax.broadcasted_iota(jnp.int32, (96, 96), 1)
    shift = jnp.sum(jnp.where(rows96 == cols96, b_out[...], 0.0), axis=1, keepdims=True)
    for copy in loads[0]:
        copy.wait()

    def forward(i, _):
        @pl.when(i == 1)
        def _():
            loads[1][0].wait()

        rows = pl.ds(pl.multiple_of(i * TILE, TILE), TILE)
        pred = jnp.broadcast_to(shift, (w_out.shape[0], TILE))
        for n in range(0, width, cut):
            if n > 0:

                @pl.when(i == 0)
                def _():
                    loads[1][1].wait()
                    load.start()

            z = jnp.dot(lat_v[rows, :], w_v[:, n : n + cut], preferred_element_type=F32)
            z = z + b_in[:, n : n + cut]
            pre[rows, n : n + cut] = z
            hidden = (z * (0.5 + 0.5 * jnp.tanh(z * (c + (c * a) * (z * z))))).astype(BF16)
            pred += lax.dot_general(w_out[:, n : n + cut], hidden, NT, preferred_element_type=F32)
        for b in range(TILE // LANE):
            ext[pl.ds(i * (TILE // LANE) + b, 96, stride=NB), :] = (
                pred[:, b * LANE : (b + 1) * LANE]
            )
        return 0

    def slopes(first, last):
        def one(i, _):
            rows = pl.ds(pl.multiple_of(i * 128, 128), 128)
            z = pre[rows, :]
            zz = z * z
            t = jnp.tanh(z * (c + (c * a) * zz))
            d = 0.5 + 0.5 * t + (0.5 * z) * (1.0 - t * t) * (c + (3.0 * c * a) * zz)
            slope[rows, :] = d.astype(BF16)
            return 0

        lax.fori_loop(first, last, one, 0)

    lax.fori_loop(0, width // TILE, forward, 0)
    field[...] = ext[0:ROWS, :].reshape(MEM, CH, LANE).astype(BF16)

    pl.semaphore_wait(
        barrier,
        MEM - 1 + 6 + has_low.astype(jnp.int32) + has_high.astype(jnp.int32)
        + jnp.where(at_edge, MEM - 1, 0),
    )

    def to_member(i):
        peer = partner(i)
        return remote(field.at[peer], recv.at[1, me], send_sem.at[i], recv_sem.at[i], peer, g)

    def from_member(i):
        src = partner(i, True)
        return remote(field.at[src], recv.at[1, src], send_sem.at[i], recv_sem.at[i], src, g)

    def halo(i, chunk, up):
        side, there = (0, g + 1) if up else (1, g - 1)
        return remote(
            recv.at[1, chunk], recv.at[0 if up else 2, chunk],
            hsend_sem.at[side, i], hrecv_sem.at[side, i], me, there,
        )

    def far(i, up):
        side = 0 if up else 1
        peer = partner(i)
        return remote(
            field.at[peer], recv.at[0 if up else 2, me],
            hsend_sem.at[side, i], hrecv_sem.at[side, i], peer, across,
        )

    def far_send(i):
        @pl.when(g == EDGE)
        def _():
            far(i, True).start()

        @pl.when(g == EDGE + 1)
        def _():
            far(i, False).start()

    def pass_on(i, chunk, up_ok, down_ok):
        @pl.when(up_ok)
        def _():
            halo(i, chunk, True).start()

        @pl.when(down_ok)
        def _():
            halo(i, chunk, False).start()

    def send(i, _):
        to_member(i).start()
        far_send(i)
        return 0

    lax.fori_loop(0, SELF, send, 0)
    far_send(SELF)
    recv[1, me] = field[me]
    pass_on(MEM, MEM, has_high, has_low)
    pass_on(SELF, me, high_near, low_near)

    slot_table(bi, posv, tabv)
    tab_copy = pltpu.make_async_copy(tabv, tab, tab_sem)
    tab_copy.start()
    load.wait()

    def weights(i, _):
        live = (i % 4 < bc[i // 32, (i // 4) % NB]).astype(jnp.int32).astype(F32)
        mb[i] = (mf[i // 32, (i // 4) % NB, i % 4] * live).astype(BF16)
        return 0

    lax.fori_loop(0, SLOTS, weights, 0, unroll=4)

    def arrive(i, _):
        i = SELF - 1 - i
        from_member(i).wait_recv()
        pass_on(i, partner(i, True), high_near, low_near)
        return 0

    lax.fori_loop(0, SELF, arrive, 0)

    xs[0:ROWS, :] = recv[1, 0:MEM].reshape(ROWS, LANE).astype(F32)
    pad = jnp.zeros((PAD - 102, LANE), BF16)
    for b in range(NB):
        blocks[NB + b] = jnp.concatenate(
            [xs[pl.ds(b, 102, stride=NB), :].astype(BF16), pad], axis=0
        )
    partial = lax.fori_loop(
        0, VD, lambda v, t: score_rows(0, v, xs, area, varw, gr, t), jnp.zeros((8, LANE), F32)
    )
    tab_copy.wait()

    def landed(i, _):
        @pl.when(has_low)
        def _():
            halo(i, 0, True).wait_recv()

        @pl.when(has_high)
        def _():
            halo(i, 0, False).wait_recv()

        return 0

    lax.fori_loop(0, MEM + 1, landed, 0)
    for side, first in ((0, 0), (2, 2 * NB)):
        ext[0:ALL, :] = recv[side].reshape(ALL, LANE).astype(F32)
        for b in range(NB):
            blocks[first + b] = jnp.concatenate(
                [ext[pl.ds(b, 102, stride=NB), :].astype(BF16), pad], axis=0
            )

    for s in range(2):
        for r in range(NB):
            i = (s * NB + r) * 4
            picked = jnp.concatenate([blocks[slot_place(bi, i + k)] for k in range(4)], axis=1)
            res = jnp.dot(
                picked, mb[i : i + 4].reshape(4 * LANE, LANE), preferred_element_type=F32
            )
            xs[pl.ds((s + 1) * ALL + r, 102, stride=NB), :] = res[:102]

    def later(i, t):
        return score_rows(1 + i // VD, i % VD, xs, area, varw, gr, t)

    def loss_copy(stage, i):
        mine = (me % 4, me // 4, g % 4, g // 4)[stage]
        return remote(
            lsum.at[stage, mine], lsum.at[stage, mine],
            lsend_sem.at[stage, i], lrecv_sem.at[stage, i], *quad(stage, i),
        )

    def loss_out(stage, value):
        mine = (me % 4, me // 4, g % 4, g // 4)[stage]
        lsum[stage, mine] = value
        for i in range(1, 4):
            loss_copy(stage, i).start()

    def loss_in(stage):
        for i in range(1, 4):
            loss_copy(stage, i).wait_recv()
        return (lsum[stage, 0] + lsum[stage, 1]) + (lsum[stage, 2] + lsum[stage, 3])

    loss_out(0, lax.fori_loop(0, 2 * VD, later, partial))

    for s in range(2):
        for r in range(NB):
            i = (s * NB + r) * 4
            rows = gr[pl.ds((s + 1) * ROWS + r, 96, stride=NB), :].astype(BF16)
            res = lax.dot_general(
                rows, mb[i : i + 4].reshape(4 * LANE, LANE), NT, preferred_element_type=F32
            )
            for k in range(4):
                contrib[i + k] = res[:, k * LANE : (k + 1) * LANE]

    def run(t, acc):
        acc = acc * tab[FLAG, t].astype(F32) + contrib[tab[ORDER, t]]
        runs[t] = acc
        return acc

    lax.fori_loop(0, SLOTS, run, jnp.zeros((96, LANE), F32), unroll=4)

    def spread(first):
        for q in range(first, first + NB):
            e = runs[tab[LAST, q]] * tab[VALID, q].astype(F32)
            ext[pl.ds((q // NB) * ROWS + q % NB, 96, stride=NB), :] = e

    def rim(q, up):
        side, there = (0, g + 1) if up else (1, g - 1)
        some = pl.ds(q * 4, 4)
        return remote(
            rimsend.at[side, some], rimrecv.at[side, some],
            rsend_sem.at[side, q], rrecv_sem.at[side, q], me, there,
        )

    def far_rim(i, side):
        peer = partner(i)
        return remote(
            rimsend.at[side, peer], zrim.at[me], esend_sem.at[i], erecv_sem.at[i], peer, across
        )

    def far_rims(side):
        def one(i, _):
            far_rim(i, side).start()
            return 0

        lax.fori_loop(0, MEM, one, 0)

    spread(0)
    rimsend[1] = ext[0:ROWS, :].reshape(MEM, CH, LANE).astype(BF16)

    @pl.when(low_near)
    def _():
        for q in range(4):
            rim(q, False).start()

    @pl.when(g == EDGE + 1)
    def _():
        far_rims(1)

    spread(2 * NB)
    rimsend[0] = ext[2 * ROWS : 3 * ROWS, :].reshape(MEM, CH, LANE).astype(BF16)

    @pl.when(high_near)
    def _():
        for q in range(4):
            rim(q, True).start()

    @pl.when(g == EDGE)
    def _():
        far_rims(0)

    spread(NB)

    loss_out(1, loss_in(0))
    slopes(0, 8)
    loss_out(2, loss_in(1))

    def to_owner(i):
        peer = partner(i)
        return remote(fsend.at[peer], zrecv.at[me], zsend_sem.at[i], zrecv_sem.at[i], peer, g)

    for q in range(4):

        @pl.when(low_near)
        def _():
            rim(q, True).wait_recv()

        @pl.when(high_near)
        def _():
            rim(q, False).wait_recv()

        at = 4 * q * CH
        value = gr[at : at + 4 * CH, :] + ext[ROWS + at : ROWS + at + 4 * CH, :]
        some = slice(4 * q, 4 * q + 4)
        value = value + rimrecv[0, some].reshape(4 * CH, LANE).astype(F32)
        value = value + rimrecv[1, some].reshape(4 * CH, LANE).astype(F32)
        fsend[some] = value.reshape(4, CH, LANE).astype(BF16)
        turn = (q - me // 4 + 4) % 4
        for kind in range(4):
            i = kind * 4 + (turn + 3) % 4

            @pl.when(i < SELF)
            def _():
                to_owner(i).start()

    zrecv[me] = fsend[me]
    loss_out(3, loss_in(2))

    def sent(i, _):
        @pl.when(has_high)
        def _():
            halo(i, 0, True).wait_send()

        @pl.when(has_low)
        def _():
            halo(i, 0, False).wait_send()

        return 0

    lax.fori_loop(0, MEM + 1, sent, 0)

    def gone(i, _):
        to_member(i).wait_send()
        return 0

    lax.fori_loop(0, SELF, gone, 0)

    @pl.when(at_edge)
    def _():
        def one(i, _):
            far_rim(i, 0).wait_send()
            return 0

        lax.fori_loop(0, MEM, one, 0)

    for q in range(4):

        @pl.when(high_near)
        def _():
            rim(q, True).wait_send()

        @pl.when(low_near)
        def _():
            rim(q, False).wait_send()


    def owned(i, _):
        src = partner(i, True)
        remote(
            fsend.at[src], zrecv.at[src], zsend_sem.at[i], zrecv_sem.at[i], src, g
        ).wait_recv()
        return 0

    lax.fori_loop(0, SELF, owned, 0)
    ext[0:ROWS, :] = zrecv[...].reshape(ROWS, LANE).astype(F32)

    @pl.when(at_edge)
    def _():
        def one(i, _):
            src = partner(i, True)
            remote(
                rimsend.at[0, src], zrim.at[src], esend_sem.at[i], erecv_sem.at[i], src, across
            ).wait_recv()
            return 0

        lax.fori_loop(0, MEM, one, 0)
        ext[0:ROWS, :] += zrim[...].reshape(ROWS, LANE).astype(F32)

    stores = [
        pltpu.make_async_copy(
            lat_v.at[pl.ds(n * TILE, TILE), :], out.at[pl.ds(n * TILE, TILE), :], out_sem.at[n]
        )
        for n in range(2)
    ]

    def backward(i, _):
        rows = pl.ds(pl.multiple_of(i * TILE, TILE), TILE)
        grad = jnp.concatenate(
            [
                ext[pl.ds(i * (TILE // LANE) + b, 96, stride=NB), :].astype(BF16)
                for b in range(TILE // LANE)
            ],
            axis=1,
        )
        back = []
        for n in range(0, width, cut):
            h = lax.dot_general(
                grad, w_out[:, n : n + cut], (((0,), (0,)), ((), ())), preferred_element_type=F32
            )
            back.append((h * slope[rows, n : n + cut].astype(F32)).astype(BF16))
        back = jnp.concatenate(back, axis=1)
        lat_v[rows, :] = lax.dot_general(back, w_v[...], NT, preferred_element_type=F32).astype(BF16)
        for n in range(2):

            @pl.when(i == n)
            def _():
                stores[n].start()

        return 0

    lax.fori_loop(0, 2, backward, 0)

    def rest(i, _):
        to_owner(i).wait_send()
        return 0

    lax.fori_loop(0, SELF, rest, 0)
    points = lat_v.shape[0]
    loss[0, 0] = jnp.sum(loss_in(3)) * (1.0 / (3 * 96 * points * MEM))

    for stage in range(4):
        for i in range(1, 4):
            loss_copy(stage, i).wait_send()
    for copy in stores:
        copy.wait()


def copy_kernel(x, out, held, in_sem, out_sem):
    count = in_sem.shape[0]
    size = x.shape[0] // count
    some = [pl.ds(n * size, size) for n in range(count)]
    ins = [
        pltpu.make_async_copy(x.at[rows], held.at[rows], in_sem.at[n])
        for n, rows in enumerate(some)
    ]
    outs = [
        pltpu.make_async_copy(held.at[rows], out.at[rows], out_sem.at[n])
        for n, rows in enumerate(some)
    ]
    for copy in ins:
        copy.start()
    for first, second in zip(ins, outs):
        first.wait()
        second.start()
    for copy in outs:
        copy.wait()


def on_device(latents, w_in, b_in, w_out, b_out, target, area_weight, var_weight,
              smoothers, block_index, block_count):
    points = latents.shape[1]
    lat = latents.reshape(points, -1)
    width = w_in.shape[1]
    smem = pl.BlockSpec(memory_space=pltpu.SMEM)
    anywhere = pl.BlockSpec(memory_space=pl.ANY)
    dma = pltpu.SemaphoreType.DMA
    some = dma((MEM,))
    chunks = (MEM, CH, LANE)
    grad, loss = pl.pallas_call(
        decoder_kernel,
        out_shape=(
            jax.ShapeDtypeStruct(lat.shape, BF16),
            jax.ShapeDtypeStruct((1, 1), F32),
        ),
        in_specs=[anywhere] * 11,
        out_specs=(anywhere, smem),
        scratch_shapes=[
            pltpu.SMEM((2, 4, NB), jnp.int32),
            pltpu.SMEM((2, NB), jnp.int32),
            pltpu.SMEM((VD,), F32),
            pltpu.VMEM((1, width), F32),
            pltpu.VMEM((96, width), BF16),
            pltpu.VMEM((1, 96), F32),
            pltpu.VMEM((VD, points), F32),
            pltpu.VMEM((NB, LANE), F32),
            dma((8,)),
            pltpu.VMEM((4, 4, 8, LANE), F32),
            pltpu.VMEM(lat.shape, BF16),
            pltpu.VMEM(w_in.shape, BF16),
            pltpu.VMEM((points, width), F32),
            pltpu.VMEM((points, width), BF16),
            pltpu.VMEM(chunks, BF16),
            pltpu.VMEM((3, MEM + 1, CH, LANE), BF16),
            pltpu.VMEM((3 * ALL, LANE), F32),
            pltpu.VMEM((3 * NB, PAD, LANE), BF16),
            pltpu.VMEM(smoothers.shape, F32),
            pltpu.VMEM((SLOTS, LANE, LANE), BF16),
            pltpu.VMEM((3 * ROWS, LANE), F32),
            pltpu.VMEM((SLOTS, 96, LANE), F32),
            pltpu.VMEM((SLOTS, 96, LANE), F32),
            pltpu.VMEM((3 * ROWS, LANE), F32),
            pltpu.VMEM((2,) + chunks, BF16),
            pltpu.VMEM((2,) + chunks, BF16),
            pltpu.VMEM(chunks, BF16),
            pltpu.VMEM(chunks, BF16),
            pltpu.VMEM(chunks, BF16),
            pltpu.VMEM((SLOTS, LANE), jnp.int32),
            pltpu.VMEM((8, LANE), jnp.int32),
            pltpu.SMEM((8, LANE), jnp.int32),
            dma((4,)), dma((2,)), dma, dma, some, some,
            dma((2, MEM + 1)), dma((2, MEM + 1)), dma((2, 4)), dma((2, 4)),
            some, some, some, some, dma((4, 4)), dma((4, 4)),
        ],
        compiler_params=pltpu.CompilerParams(
            collective_id=0, has_side_effects=True, vmem_limit_bytes=60 * 1024 * 1024
        ),
    )(
        jnp.transpose(block_index, (0, 2, 1)), block_count, var_weight, lat, w_in,
        b_in.reshape(1, -1), w_out.T, b_out.reshape(1, -1), target,
        area_weight.reshape(NB, LANE), smoothers,
    )
    result = pl.pallas_call(
        copy_kernel,
        out_shape=jax.ShapeDtypeStruct(lat.shape, BF16),
        in_specs=[anywhere],
        out_specs=anywhere,
        scratch_shapes=[pltpu.VMEM(lat.shape, BF16), dma((4,)), dma((4,))],
        compiler_params=pltpu.CompilerParams(vmem_limit_bytes=62 * 1024 * 1024),
    )(grad)
    return result.reshape(latents.shape), loss.reshape(())


def solution(mesh):
    in_specs = (
        P("member", "grid", None), P(), P(), P(), P(),
        P("member", "grid"), P("grid"), P("member"),
        P(None, "grid", None, None, None), P(None, "grid", None), P(None, "grid"),
    )
    return jax.shard_map(
        on_device, mesh=mesh, in_specs=in_specs,
        out_specs=(P("member", "grid", None), P()), check_vma=False,
    )
```
